32 devices in a mesh: groups: 2 (over x), tile: 16 (over z, y, core).
Axes of the slice: x: 2, y: 2, z: 4, core: 2. Of those that a mesh axis runs over, the one named last changes fastest.
Arguments:
- strain: bfloat16 [12288, 2, 4096], P(('groups', 'tile')), parts along dimension 0, may hold values from -6 to 6
- tile_pairs: int32 [96, 2], P(('groups', 'tile')), parts along dimension 0, may hold values from 0 to 47, as said below
- tile_count: int32 [32], P(('groups', 'tile')), parts along dimension 0, may hold values from 2 to 3, as said below
Outputs:
- correlations: bfloat16 [96, 128, 8192], P(('groups', 'tile')), parts along dimension 0
The draws below stay inside these ranges and needn't reach their ends.
There are 2 independent parts, one for each index of `groups`. The reference program is written for one: setup_inputs(seed, part) draws one part's arguments, and reference() takes and returns one part's arrays. A program takes and returns all parts, laid end to end along the dimension named above; each array names one. Nothing has to cross between parts.
Inputs may be any that keep to these rules, and one draw needn't show every extreme that they name: `tile_pairs`: row k holds row block k and a column block from k to k + 6; where k mod 3 is 0, the column block is k + 6, where it is 1, k + 3, or the last block where that lies beyond it. `tile_count`: some device has all 3 tiles live in every draw.
All inputs are finite; a program needn't handle non-finite values.
Results may differ from the reference program's by a relative error of at most 0.0075.
Values may be sent and summed in bfloat16 or wider, within the bound.
No kernel may reach another device: no remote copies, remote signals or barrier semaphores. Data moves between devices by JAX's collectives and lax.ppermute only.
A program may use at most 128 MiB of HBM per device.

```python
import math
import jax
import jax.numpy as jnp
from jax import lax

CH = 128
WIN = 4096
BAND = 256
BIN0 = 60
SMOOTH = 64
LAGS = 64
WINS = 2
BLK_DEV = 3
REACH = 6
NBLK = 48
NCHAN = 6144
N_TILE = 16


def draw_tile_pairs(key, part):
    key = jax.random.fold_in(key, 11)
    rows = jnp.arange(NBLK, dtype=jnp.int32)
    offsets = jax.random.randint(key, (NBLK,), 0, REACH + 1)
    offsets = jnp.where(rows % BLK_DEV == 0, REACH, offsets)
    offsets = jnp.where(rows % BLK_DEV == 1, BLK_DEV, offsets)
    cols = jnp.minimum(rows + offsets, NBLK - 1)
    return jnp.stack([rows, cols], 1).astype(jnp.int32)


def draw_tile_count(key, part):
    key = jax.random.fold_in(key, 23)
    first_key, second_key = jax.random.split(key)
    counts = jax.random.randint(first_key, (N_TILE,), 2, BLK_DEV + 1)
    fullest = jax.random.randint(second_key, (), 0, N_TILE)
    places = jnp.arange(N_TILE, dtype=jnp.int32)
    return jnp.where(places == fullest, BLK_DEV, counts).astype(jnp.int32)


def level_of(rng, shape, cuts, smallest, high):
    level, own = 1.0, jax.random.fold_in(rng, 6)
    for dim, parts in cuts:
        draws = jnp.exp(jax.random.uniform(jax.random.fold_in(own, dim), (parts,), jnp.float32, smallest / len(cuts), high / len(cuts)))
        level = level * jnp.repeat(draws, shape[dim] // parts).reshape([-1 if axis == dim else 1 for axis in range(len(shape))])
    return level


def bell_draw(own_key, dims, deviation, bound, shards=(), kind=jnp.bfloat16):
    drawn = jax.random.normal(own_key, dims, jnp.float32) * deviation
    if len(shards) > 0:
        drawn = level_of(own_key, dims, shards, -0.22, 0.18) * drawn
    return jnp.clip(drawn, min=-bound, max=bound).astype(kind)


def setup_inputs(seed: int = 0, part: int = 0) -> dict:
    splits = jax.random.split(jax.random.key(seed), 4)
    own_keys = jax.random.split(jax.random.fold_in(splits[3], part), 4)
    return {
        "strain": bell_draw(own_keys[0], (NCHAN, WINS, WIN), 1.0, 6.0, ((0, 16),)),
        "tile_pairs": draw_tile_pairs(jax.random.fold_in(jax.random.fold_in(splits[3], part), 71), part),
        "tile_count": draw_tile_count(jax.random.fold_in(jax.random.fold_in(splits[3], part), 71), part),
    }


def dft_table(n_win, first, band):
    times = jnp.arange(n_win, dtype=jnp.int32)[:, None]
    freqs = first + jnp.arange(band, dtype=jnp.int32)[None, :]
    phase = times * freqs % n_win
    angle = phase.astype(jnp.float32) * (2.0 * math.pi / n_win)
    return jnp.concatenate([jnp.cos(angle), -jnp.sin(angle)], 1).astype(jnp.bfloat16)

def lag_table(n_win, first, band, lags):
    freqs = first + jnp.arange(band, dtype=jnp.int32)[:, None]
    shifts = jnp.arange(lags, dtype=jnp.int32)[None, :] - lags // 2
    phase = freqs * shifts % n_win
    angle = phase.astype(jnp.float32) * (2.0 * math.pi / n_win)
    return jnp.concatenate([jnp.cos(angle), -jnp.sin(angle)], 0).astype(jnp.bfloat16)

def whiten(strain, table, band, smooth):
    chans, wins, n_win = strain.shape
    spectrum = jnp.dot(strain.reshape(chans * wins, n_win), table, preferred_element_type=jnp.float32)
    real_part = spectrum[:, :band]
    imag_part = spectrum[:, band:]
    energy = (real_part * real_part + imag_part * imag_part).reshape(chans * wins, band // smooth, smooth)
    power = lax.optimization_barrier(jnp.mean(energy, axis=2, keepdims=True)) + 1e-06
    factor = jnp.broadcast_to(lax.rsqrt(power), energy.shape).reshape(chans * wins, band)
    whitened = jnp.concatenate([real_part * factor, imag_part * factor], 1).astype(jnp.bfloat16)
    return whitened.reshape(chans, wins, 2 * band)

def correlate(row_block, col_block, lagtab, band, scale):
    row_re = row_block[:, :, :band].astype(jnp.float32)
    row_im = row_block[:, :, band:].astype(jnp.float32)
    col_re = col_block[:, :, :band].astype(jnp.float32)
    col_im = col_block[:, :, band:].astype(jnp.float32)
    cross_re = jnp.einsum('iwf,jwf->ijf', row_re, col_re) + jnp.einsum('iwf,jwf->ijf', row_im, col_im)
    cross_im = jnp.einsum('iwf,jwf->ijf', row_im, col_re) - jnp.einsum('iwf,jwf->ijf', row_re, col_im)
    cross = jnp.concatenate([cross_re, cross_im], 2).astype(jnp.bfloat16)
    chans = row_block.shape[0]
    corr = jnp.dot(cross.reshape(chans * chans, 2 * band), lagtab, preferred_element_type=jnp.float32) * scale
    return corr.reshape(chans, -1)

def reference(strain, tile_pairs, tile_count):
    table = dft_table(WIN, BIN0, BAND)
    lagtab = lag_table(WIN, BIN0, BAND, LAGS)
    whitened = whiten(strain, table, BAND, SMOOTH).reshape(NBLK, CH, WINS, 2 * BAND)
    scale = 1.0 / math.sqrt(WINS * BAND)

    def one_tile(index):
        row_block = whitened[tile_pairs[index, 0]]
        col_block = whitened[tile_pairs[index, 1]]
        corr = correlate(row_block, col_block, lagtab, BAND, scale)
        live = tile_count[index // BLK_DEV] > index % BLK_DEV
        return jnp.where(live, corr, jnp.zeros_like(corr)).astype(jnp.bfloat16)
    return lax.map(one_tile, jnp.arange(NBLK, dtype=jnp.int32))
```

```python
import functools
import math

import jax
import jax.numpy as jnp
import numpy as np
from jax import lax
from jax.experimental import pallas as pl
from jax.experimental.pallas import tpu as pltpu
from jax.sharding import PartitionSpec as P

CH = 128
WIN = 4096
BAND = 256
BIN0 = 60
SMOOTH = 64
LAGS = 64
FINE = 8
COARSE = LAGS // FINE
GROUPS = 4
BF16 = jnp.bfloat16
F32 = jnp.float32


def bin_order():
    return np.concatenate([np.arange(0, BAND, 2), np.arange(1, BAND, 2)])


def dft_tables():
    times = np.arange(WIN // 2, dtype=np.int64)[:, None]
    tables = []
    for parity in range(2):
        freqs = BIN0 + np.arange(parity, BAND, 2, dtype=np.int64)[None, :]
        angle = (times * freqs % WIN) * (2.0 * math.pi / WIN)
        tables.append(np.concatenate([np.cos(angle), -np.sin(angle)], 1))
    return np.stack(tables).astype(BF16)


def mean_table():
    group = bin_order() // SMOOTH
    return ((group[:, None] == group[None, :]) / SMOOTH).astype(BF16)


def phase_tables(scale):
    freqs = (BIN0 + bin_order())[None, :]
    coarse = FINE * np.arange(COARSE)[:, None] - LAGS // 2
    fine = np.arange(FINE)[:, None]
    step = 2.0 * math.pi / WIN
    a = np.concatenate([np.cos(coarse * freqs * step), np.sin(coarse * freqs * step)], 1) * scale
    b = np.concatenate([np.cos(fine * freqs * step), np.sin(fine * freqs * step)], 1)
    return a.astype(np.float32), b.astype(np.float32)


def dft_kernel(block, x_hbm, table_hbm, mean_ref, out_ref, xs, tab, acc, wide, x_sem, t_sem):
    tiles = WIN // 128
    half = tiles // 2
    per = half // GROUPS
    depth = per * 128

    def x_copy(t):
        return pltpu.make_async_copy(
            x_hbm.at[pl.ds(block * CH, CH), :, pl.ds(t * 128, 128)], xs.at[t], x_sem.at[t]
        )

    def t_copy(g):
        rows = pl.ds(g * depth, depth)
        return pltpu.make_async_copy(table_hbm.at[:, rows, :], tab.at[:, rows, :], t_sem.at[g])

    for g in range(GROUPS):
        for t in range(g * per, (g + 1) * per):
            x_copy(t).start()
            x_copy(t + half).start()
        t_copy(g).start()
    flat = xs.reshape(tiles, 2 * CH, 128)
    for g in range(GROUPS):
        sums, differences = [], []
        for t in range(g * per, (g + 1) * per):
            x_copy(t).wait()
            x_copy(t + half).wait()
            first, second = flat[t], flat[t + half]
            sums.append(first + second)
            differences.append(first - second)
        t_copy(g).wait()
        for parity, left in enumerate((sums, differences)):
            part = jnp.dot(
                jnp.concatenate(left, 1),
                tab[parity, g * depth : (g + 1) * depth, :],
                preferred_element_type=F32,
            )
            if g == 0:
                acc[parity] = part
            else:
                acc[parity] += part
    energy = []
    for parity in range(2):
        re = acc[parity, :, :128]
        im = acc[parity, :, 128:]
        energy.append(re * re + im * im)
    energy = jnp.concatenate(energy, 1)
    high = energy.astype(BF16)
    low = (energy - high.astype(F32)).astype(BF16)
    power = jnp.dot(high, mean_ref[...], preferred_element_type=F32)
    power += jnp.dot(low, mean_ref[...], preferred_element_type=F32)
    factor = lax.rsqrt(power + 1e-06)
    for parity in range(2):
        scaled = factor[:, parity * 128 : (parity + 1) * 128]
        wide[parity] = acc[parity, :, :128] * scaled
        wide[2 + parity] = acc[parity, :, 128:] * scaled
    for w in range(2):
        for q in range(4):
            column = (w * 4 + q) * 128
            out_ref[:, column : column + 128] = wide[q, pl.ds(w, CH, stride=2), :].astype(BF16)


def dft_block(strain, table, mean, block):
    wins = strain.shape[1]
    return pl.pallas_call(
        functools.partial(dft_kernel, block),
        out_shape=jax.ShapeDtypeStruct((CH, wins * 2 * BAND), BF16),
        in_specs=[
            pl.BlockSpec(memory_space=pl.ANY),
            pl.BlockSpec(memory_space=pl.ANY),
            pl.BlockSpec(memory_space=pltpu.VMEM),
        ],
        out_specs=pl.BlockSpec(memory_space=pltpu.VMEM),
        scratch_shapes=[
            pltpu.VMEM((WIN // 128, CH, wins, 128), BF16),
            pltpu.VMEM((2, WIN // 2, BAND), BF16),
            pltpu.VMEM((2, CH * wins, BAND), F32),
            pltpu.VMEM((4, CH * wins, 128), F32),
            pltpu.SemaphoreType.DMA((WIN // 128,)),
            pltpu.SemaphoreType.DMA((GROUPS,)),
        ],
        compiler_params=pltpu.CompilerParams(vmem_limit_bytes=32 * 2**20),
        cost_estimate=pl.CostEstimate(
            flops=2 * CH * wins * WIN * BAND, bytes_accessed=2 * CH * wins * WIN + 2 * WIN * BAND,
            transcendentals=0,
        ),
        name=f"spectrum_{block}",
    )(strain, table, mean)


def corr_kernel(slot, names, *refs):
    which_ref, row_ref, atab_ref, btab_ref = refs[:4]
    cands = refs[4 : 4 + names]
    out_ref, col, acoef, bcoef, prod, sem = refs[-6:]
    chunk = pl.program_id(0)
    live = which_ref[1] > 0
    js = 256 // FINE

    @pl.when(jnp.logical_and(live, chunk == 0))
    def _():
        for n, cand in enumerate(cands):

            @pl.when(which_ref[0] == n)
            def _():
                copy = pltpu.make_async_copy(cand, col, sem)
                copy.start()
                copy.wait()

        for w in range(2):
            for p in range(2):
                re = row_ref[:, (w * 4 + p) * 128 : (w * 4 + p + 1) * 128].astype(F32)
                im = row_ref[:, (w * 4 + 2 + p) * 128 : (w * 4 + 3 + p) * 128].astype(F32)
                for a in range(COARSE):
                    cos = atab_ref[a : a + 1, p * 128 : (p + 1) * 128]
                    sin = atab_ref[a : a + 1, (2 + p) * 128 : (3 + p) * 128]
                    rows = slice(a * CH, (a + 1) * CH)
                    acoef[rows, (w * 4 + p) * 128 : (w * 4 + p + 1) * 128] = (
                        re * cos - im * sin
                    ).astype(BF16)
                    acoef[rows, (w * 4 + 2 + p) * 128 : (w * 4 + 3 + p) * 128] = (
                        re * sin + im * cos
                    ).astype(BF16)

    @pl.when(live)
    def _():
        part = col[pl.ds(pl.multiple_of(chunk * js, js), js), :].astype(F32)
        for w in range(2):
            for p in range(2):
                re_cols = slice((w * 4 + p) * 128, (w * 4 + p + 1) * 128)
                im_cols = slice((w * 4 + 2 + p) * 128, (w * 4 + 3 + p) * 128)
                cos = btab_ref[:, p * 128 : (p + 1) * 128]
                sin = btab_ref[:, (2 + p) * 128 : (3 + p) * 128]
                for place in range(0, js, 2):
                    res, ims = [], []
                    for pos in (place, place + 1):
                        v, inner = divmod(pos, 16)
                        jj, q = divmod(inner, 8)
                        j = v * 16 + 2 * q + jj
                        re = part[j : j + 1, re_cols]
                        im = part[j : j + 1, im_cols]
                        res.append(re * cos + im * sin)
                        ims.append(im * cos - re * sin)
                    rows = slice(place * FINE, (place + 2) * FINE)
                    bcoef[rows, re_cols] = jnp.concatenate(res, 0).astype(BF16)
                    bcoef[rows, im_cols] = jnp.concatenate(ims, 0).astype(BF16)
        prod[...] = lax.dot_general(
            acoef[...], bcoef[...], (((1,), (1,)), ((), ())), preferred_element_type=F32
        ).astype(BF16)
        lane = lax.broadcasted_iota(jnp.int32, (CH, 128), 1)
        for v in range(2):
            x = [prod[a * CH : (a + 1) * CH, v * 128 : (v + 1) * 128] for a in range(COARSE)]
            for bit in (1, 2, 4):
                upper = (lane // FINE) & bit != 0
                for a in range(COARSE):
                    if a & bit == 0:
                        lo, hi = x[a], x[a | bit]
                        x[a] = jnp.where(upper, pltpu.roll(hi, FINE * bit, 1), lo)
                        x[a | bit] = jnp.where(upper, hi, pltpu.roll(lo, 128 - FINE * bit, 1))
            for q in range(8):
                column = v * 1024 + q * 128
                out_ref[0, :, column : column + 128] = x[q]

    @pl.when(jnp.logical_not(live))
    def _():
        out_ref[...] = jnp.zeros_like(out_ref)


def corr_tile(slot, blocks, which, row, tables, cands, buffer):
    js = 256 // FINE
    chunks = CH // js
    in_specs = [
        pl.BlockSpec(memory_space=pltpu.SMEM),
        pl.BlockSpec(memory_space=pltpu.VMEM),
        pl.BlockSpec(memory_space=pltpu.VMEM),
        pl.BlockSpec(memory_space=pltpu.VMEM),
    ] + [pl.BlockSpec(memory_space=pl.ANY) for _ in cands]
    operands = [which, row, *tables, *cands]
    aliases = {}
    if buffer is not None:
        aliases = {len(operands): 0}
        operands.append(buffer)
        in_specs.append(pl.BlockSpec(memory_space=pl.ANY))
    depth = row.shape[1]
    return pl.pallas_call(
        functools.partial(corr_kernel, slot, len(cands)),
        grid=(chunks,),
        out_shape=jax.ShapeDtypeStruct((blocks, CH, CH * LAGS), BF16),
        in_specs=in_specs,
        out_specs=pl.BlockSpec((1, CH, js * LAGS), lambda c: (slot, 0, c)),
        scratch_shapes=[
            pltpu.VMEM((CH, depth), BF16),
            pltpu.VMEM((COARSE * CH, depth), BF16),
            pltpu.VMEM((js * FINE, depth), BF16),
            pltpu.VMEM((COARSE * CH, js * FINE), BF16),
            pltpu.SemaphoreType.DMA,
        ],
        input_output_aliases=aliases,
        compiler_params=pltpu.CompilerParams(vmem_limit_bytes=32 * 2**20),
        cost_estimate=pl.CostEstimate(
            flops=2 * CH * CH * LAGS * depth, bytes_accessed=2 * CH * CH * LAGS, transcendentals=0
        ),
        name=f"lags_{slot}",
    )(*operands)


def body(strain, tile_pairs, tile_count):
    blocks = strain.shape[0] // CH
    wins = strain.shape[1]
    size = lax.axis_size("tile")
    me = lax.axis_index("tile")
    table = jnp.asarray(dft_tables())
    mean = jnp.asarray(mean_table())
    tables = [jnp.asarray(t) for t in phase_tables(1.0 / math.sqrt(wins * BAND))]
    ahead1 = [(i, i - 1) for i in range(1, size)]
    ahead2 = [(i, i - 2) for i in range(2, size)]
    swap = [(i, i ^ 1) for i in range(size)]
    base = me * blocks

    last = tile_pairs[blocks - 1 :, 1]
    want1 = lax.ppermute(last, "tile", [(i - 1, i) for i in range(1, size)])[0] - base
    want2 = lax.ppermute(last, "tile", [(i - 2, i) for i in range(2, size)])[0] - base

    w0 = dft_block(strain, table, mean, 0)
    far0 = lax.ppermute(w0, "tile", ahead2)
    w1 = dft_block(strain, table, mean, 1)
    near1 = lax.ppermute(w1, "tile", ahead1)
    w2 = dft_block(strain, table, mean, 2)

    def pick(index):
        return jnp.where(index == 0, w0, jnp.where(index == 1, w1, w2))

    other = lax.ppermute(jnp.stack([pick(want1), w2]), "tile", swap)
    here = jnp.logical_or(me % 2 == 0, want2 >= 0)
    far = lax.ppermute(jnp.where(here, pick(want2), other[0]), "tile", ahead2)

    cols = tile_pairs[:, 1] - base
    step = cols // blocks
    count = tile_count[0]

    def which(slot, index):
        live = (count > slot).astype(jnp.int32)
        return jnp.stack([index.astype(jnp.int32), live])

    out = corr_tile(0, blocks, which(0, step[0]), w0, tables, [w2, other[1], far0], None)
    out = corr_tile(1, blocks, which(1, jnp.minimum(step[1], 1)), w1, tables, [w2, near1], out)
    odd = me % 2
    source = jnp.where(odd == 1, 2 * jnp.minimum(step[2], 1), step[2])
    return corr_tile(2, blocks, which(2, source), w2, tables, [w2, other[0], far], out)


def solution(mesh):
    in_specs = (
        P(("groups", "tile"), None, None),
        P(("groups", "tile"), None),
        P(("groups", "tile")),
    )
    out_specs = P(("groups", "tile"), None, None)
    return jax.shard_map(body, mesh=mesh, in_specs=in_specs, out_specs=out_specs, check_vma=False)
```

```python
import functools
import math

import jax
import jax.numpy as jnp
import numpy as np
from jax import lax
from jax.experimental import pallas as pl
from jax.experimental.pallas import tpu as pltpu
from jax.sharding import PartitionSpec as P

CH = 128
WIN = 4096
BAND = 256
BIN0 = 60
SMOOTH = 64
LAGS = 64
FINE = 8
COARSE = LAGS // FINE
ROWS = 16
TOGETHER = 8
VMEM_BYTES = 60 * 2**20
BF16 = jnp.bfloat16
F32 = jnp.float32


def bin_order():
    return np.concatenate([np.arange(0, BAND, 2), np.arange(1, BAND, 2)])


def dft_tables():
    times = np.arange(WIN // 2, dtype=np.int64)[:, None]
    tables = []
    for parity in range(2):
        freqs = BIN0 + np.arange(parity, BAND, 2, dtype=np.int64)[None, :]
        angle = (times * freqs % WIN) * (2.0 * math.pi / WIN)
        tables.append(np.concatenate([np.cos(angle), -np.sin(angle)], 1))
    return np.stack(tables).astype(BF16)


def mean_table():
    group = bin_order() // SMOOTH
    return ((group[:, None] == group[None, :]) / SMOOTH).astype(BF16)


def fold_table(wins):
    inner = ROWS // wins
    row = np.arange(2 * inner * TOGETHER * wins)
    sign, s, c, w = np.unravel_index(row, (2, inner, TOGETHER, wins))
    table = np.zeros((row.size, row.size), np.float32)
    for half in range(2):
        column = np.ravel_multi_index((c, half + 0 * c, s, w), (TOGETHER, 2, inner, wins))
        table[row, column] = np.where((sign == 1) & (half == 1), -1.0, 1.0)
    return table.astype(BF16)


def phase_tables(scale):
    freqs = (BIN0 + bin_order())[None, :]
    coarse = FINE * np.arange(1, COARSE // 2 + 1)[:, None]
    fine = np.arange(FINE)[:, None]
    step = 2.0 * math.pi / WIN
    a = np.concatenate([np.cos(coarse * freqs * step), np.sin(coarse * freqs * step)], 1) * scale
    b = np.concatenate([np.cos(fine * freqs * step), np.sin(fine * freqs * step)], 1)
    return a.astype(np.float32), b.astype(np.float32)


def transform(x_ref, fold_ref, mean_ref, tab_ref, left, acc, wide, m, put):
    wins = ROWS // 8
    for pair in range(0, CH // TOGETHER, 2):
        sides = []
        for g in (pair, pair + 1):
            rows = x_ref[g * TOGETHER : (g + 1) * TOGETHER, :, 0]
            sides.append(rows.reshape(TOGETHER * 2 * ROWS, 128))
        folded = jnp.dot(
            fold_ref[...], jnp.concatenate(sides, 1), preferred_element_type=F32
        ).astype(BF16)
        size = TOGETHER * wins
        for sign in range(2):
            for s in range(8):
                piece = folded[(sign * 8 + s) * size : (sign * 8 + s + 1) * size]
                for n, g in enumerate((pair, pair + 1)):
                    left[sign, g * size : (g + 1) * size, s * 128 : (s + 1) * 128] = piece[
                        :, n * 128 : (n + 1) * 128
                    ]
    parts = [
        jnp.dot(left[sign], tab_ref[sign], preferred_element_type=F32) for sign in range(2)
    ]

    @pl.when(m == 0)
    def _():
        for sign in range(2):
            acc[sign] = parts[sign]

    @pl.when(m == 1)
    def _():
        spec = [acc[sign] + parts[sign] for sign in range(2)]
        energy = [s[:, :128] * s[:, :128] + s[:, 128:] * s[:, 128:] for s in spec]
        energy = jnp.concatenate(energy, 1)
        high = energy.astype(BF16)
        low = (energy - high.astype(F32)).astype(BF16)
        power = jnp.dot(high, mean_ref[...], preferred_element_type=F32)
        power += jnp.dot(low, mean_ref[...], preferred_element_type=F32)
        factor = lax.rsqrt(power + 1e-06)
        for sign in range(2):
            scaled = factor[:, sign * 128 : (sign + 1) * 128]
            wide[sign] = spec[sign][:, :128] * scaled
            wide[2 + sign] = spec[sign][:, 128:] * scaled
        for w in range(wins):
            for q in range(4):
                column = (w * 4 + q) * 128
                put(column, wide[q, pl.ds(w, CH, stride=wins), :].astype(BF16))


def first_kernel(x_ref, fold_ref, mean_ref, tab_ref, out_ref, left, acc, wide):
    def put(column, value):
        out_ref[:, column : column + 128] = value

    transform(x_ref, fold_ref, mean_ref, tab_ref, left, acc, wide, pl.program_id(1), put)


def rest_kernel(x_ref, fold_ref, mean_ref, tab_ref, w0_ref, one_ref, all_ref, left, acc, wide):
    block = pl.program_id(0)

    @pl.when(jnp.logical_and(block == 0, pl.program_id(1) == 0))
    def _():
        all_ref[0] = w0_ref[...]

    def put(column, value):
        all_ref[block + 1, :, column : column + 128] = value

        @pl.when(block == 0)
        def _():
            one_ref[:, column : column + 128] = value

    transform(x_ref, fold_ref, mean_ref, tab_ref, left, acc, wide, pl.program_id(1), put)


def spectra(kernel, view, consts, first, count, extra, outs, name):
    wins = ROWS // 8
    depth = WIN // 4
    whole = pl.BlockSpec(memory_space=pltpu.VMEM)
    return pl.pallas_call(
        kernel,
        grid=(count, 2),
        out_shape=[jax.ShapeDtypeStruct(shape, BF16) for shape in outs],
        in_specs=[
            pl.BlockSpec((CH, 2, 1, ROWS, 128), lambda b, m: (first + b, 0, m, 0, 0)),
            pl.BlockSpec((256, 256), lambda b, m: (0, 0)),
            pl.BlockSpec((BAND, BAND), lambda b, m: (0, 0)),
            pl.BlockSpec((2, depth, BAND), lambda b, m: (0, m, 0)),
        ]
        + [whole] * len(extra),
        out_specs=[whole] * len(outs),
        scratch_shapes=[
            pltpu.VMEM((2, CH * wins, depth), BF16),
            pltpu.VMEM((2, CH * wins, BAND), F32),
            pltpu.VMEM((4, CH * wins, 128), F32),
        ],
        compiler_params=pltpu.CompilerParams(vmem_limit_bytes=VMEM_BYTES),
        cost_estimate=pl.CostEstimate(
            flops=count * 4 * CH * wins * WIN * BAND,
            bytes_accessed=count * (2 * CH * wins * WIN + 2 * WIN * BAND),
            transcendentals=0,
        ),
        name=name,
    )(view, *consts, *extra)


def pick_kernel(blocks, want_ref, all_ref, other_ref, out_ref, sem):
    me = lax.axis_index("tile")
    index = want_ref[blocks - 1, 1] - me * blocks

    @pl.when(jnp.logical_or(index >= 0, me % 2 == 0))
    def _():
        copy = pltpu.make_async_copy(all_ref.at[jnp.clip(index, 0, blocks - 1)], out_ref, sem)
        copy.start()
        copy.wait()

    @pl.when(jnp.logical_and(index < 0, me % 2 == 1))
    def _():
        index2 = jnp.clip(index + blocks, 0, blocks - 1)
        copy = pltpu.make_async_copy(other_ref.at[index2], out_ref, sem)
        copy.start()
        copy.wait()


def pick(want, everything, other):
    blocks = everything.shape[0]
    return pl.pallas_call(
        functools.partial(pick_kernel, blocks),
        out_shape=jax.ShapeDtypeStruct(everything.shape[1:], BF16),
        in_specs=[
            pl.BlockSpec(memory_space=pltpu.SMEM),
            pl.BlockSpec(memory_space=pl.ANY),
            pl.BlockSpec(memory_space=pl.ANY),
        ],
        out_specs=pl.BlockSpec(memory_space=pltpu.VMEM),
        scratch_shapes=[pltpu.SemaphoreType.DMA],
        name="chosen_block",
    )(want, everything, other)


def corr_kernel(slot, blocks, scale, *refs):
    pairs_ref, count_ref, row_ref, atab_ref, btab_ref, all_ref, other_ref, far_ref = refs[:8]
    out_hbm, raw, col, acoef, b0, b1, p0, p1, obuf, in_sem, out_sem = refs[-11:]
    js = 256 // FINE
    chunks = CH // js
    live = count_ref[0] > slot
    me = lax.axis_index("tile")
    index = pairs_ref[slot, 1] - me * blocks
    even = me % 2 == 0
    own = index < blocks
    beside = jnp.logical_and(index >= blocks, jnp.logical_and(even, index < 2 * blocks))
    remote = jnp.logical_not(jnp.logical_or(own, beside))

    def out_copy(c):
        columns = pl.ds(c * js * LAGS, js * LAGS)
        return pltpu.make_async_copy(
            obuf.at[:, columns], out_hbm.at[slot, :, columns], out_sem.at[c]
        )

    @pl.when(live)
    def _():
        @pl.when(own)
        def _():
            pltpu.make_async_copy(all_ref.at[jnp.clip(index, 0, blocks - 1)], raw, in_sem).start()

        @pl.when(beside)
        def _():
            pltpu.make_async_copy(
                other_ref.at[jnp.clip(index - blocks, 0, blocks - 1)], raw, in_sem
            ).start()

        @pl.when(remote)
        def _():
            pltpu.make_async_copy(far_ref, raw, in_sem).start()

        for w in range(2):
            for p in range(2):
                re_cols = slice((w * 4 + p) * 128, (w * 4 + p + 1) * 128)
                im_cols = slice((w * 4 + 2 + p) * 128, (w * 4 + 3 + p) * 128)
                re = row_ref[0, :, re_cols].astype(F32)
                im = row_ref[0, :, im_cols].astype(F32)

                def put(a, re_value, im_value):
                    rows = slice(a * CH, (a + 1) * CH)
                    acoef[rows, re_cols] = re_value.astype(BF16)
                    acoef[rows, im_cols] = im_value.astype(BF16)

                middle = COARSE // 2
                put(middle, re * scale, im * scale)
                for n in range(1, middle + 1):
                    cos = atab_ref[n - 1 : n, p * 128 : (p + 1) * 128]
                    sin = atab_ref[n - 1 : n, (2 + p) * 128 : (3 + p) * 128]
                    rc, ic, rs, ims = re * cos, im * cos, re * sin, im * sin
                    put(middle - n, rc + ims, ic - rs)
                    if n < middle:
                        put(middle + n, rc - ims, ic + rs)
        pltpu.make_async_copy(far_ref, raw, in_sem).wait()
        for q in range(8):
            col[q] = raw[:, q * 128 : (q + 1) * 128].astype(F32)

        def build(c, b):
            for w in range(2):
                for p in range(2):
                    re_q, im_q = w * 4 + p, w * 4 + 2 + p
                    cos = btab_ref[:, p * 128 : (p + 1) * 128]
                    sin = btab_ref[:, (2 + p) * 128 : (3 + p) * 128]
                    for place in range(0, js, 2):
                        res, ims = [], []
                        for pos in (place, place + 1):
                            v, inner = divmod(pos, 16)
                            jj, q = divmod(inner, 8)
                            j = c * js + v * 16 + 2 * q + jj
                            re = col[re_q, pl.ds(j, FINE, stride=0), :]
                            im = col[im_q, pl.ds(j, FINE, stride=0), :]
                            res.append(re * cos + im * sin)
                            ims.append(im * cos - re * sin)
                        rows = slice(place * FINE, (place + 2) * FINE)
                        b[rows, re_q * 128 : (re_q + 1) * 128] = jnp.concatenate(res, 0).astype(BF16)
                        b[rows, im_q * 128 : (im_q + 1) * 128] = jnp.concatenate(ims, 0).astype(BF16)

        def multiply(b, p):
            p[...] = lax.dot_general(
                acoef[...], b[...], (((1,), (1,)), ((), ())), preferred_element_type=F32
            ).astype(BF16)

        lane = lax.broadcasted_iota(jnp.int32, (CH, 128), 1)

        def arrange(c, prod):
            for v in range(2):
                x = [prod[a * CH : (a + 1) * CH, v * 128 : (v + 1) * 128] for a in range(COARSE)]
                for bit in (1, 2, 4):
                    upper = (lane // FINE) & bit != 0
                    for a in range(COARSE):
                        if a & bit == 0:
                            lo, hi = x[a], x[a | bit]
                            x[a] = jnp.where(upper, pltpu.roll(hi, FINE * bit, 1), lo)
                            x[a | bit] = jnp.where(upper, hi, pltpu.roll(lo, 128 - FINE * bit, 1))
                for q in range(8):
                    column = c * js * LAGS + v * 1024 + q * 128
                    obuf[:, column : column + 128] = x[q]
            out_copy(c).start()

        bs, ps = (b0, b1), (p0, p1)
        build(0, b0)
        for c in range(chunks):
            multiply(bs[c % 2], ps[c % 2])
            if c + 1 < chunks:
                build(c + 1, bs[(c + 1) % 2])
            if c > 0:
                arrange(c - 1, ps[(c - 1) % 2])
        arrange(chunks - 1, ps[(chunks - 1) % 2])

    @pl.when(jnp.logical_not(live))
    def _():
        obuf[...] = jnp.zeros_like(obuf)
        for c in range(chunks):
            out_copy(c).start()

    for c in range(chunks):
        out_copy(c).wait()


def corr_tile(slot, scale, pairs, count, tables, everything, other, far, buffer):
    js = 256 // FINE
    chunks = CH // js
    blocks, _, depth = everything.shape
    in_specs = [
        pl.BlockSpec(memory_space=pltpu.SMEM),
        pl.BlockSpec(memory_space=pltpu.SMEM),
        pl.BlockSpec((1, CH, depth), lambda i: (slot, 0, 0)),
        pl.BlockSpec(memory_space=pltpu.VMEM),
        pl.BlockSpec(memory_space=pltpu.VMEM),
    ] + [pl.BlockSpec(memory_space=pl.ANY)] * 3
    operands = [pairs, count, everything, *tables, everything, other, far]
    aliases = {}
    if buffer is not None:
        aliases = {len(operands): 0}
        operands.append(buffer)
        in_specs.append(pl.BlockSpec(memory_space=pl.ANY))
    return pl.pallas_call(
        functools.partial(corr_kernel, slot, blocks, scale),
        grid=(1,),
        out_shape=jax.ShapeDtypeStruct((blocks, CH, CH * LAGS), BF16),
        in_specs=in_specs,
        out_specs=pl.BlockSpec(memory_space=pl.ANY),
        scratch_shapes=[
            pltpu.VMEM((CH, depth), BF16),
            pltpu.VMEM((8, CH, 128), F32),
            pltpu.VMEM((COARSE * CH, depth), BF16),
            pltpu.VMEM((js * FINE, depth), BF16),
            pltpu.VMEM((js * FINE, depth), BF16),
            pltpu.VMEM((COARSE * CH, js * FINE), BF16),
            pltpu.VMEM((COARSE * CH, js * FINE), BF16),
            pltpu.VMEM((CH, CH * LAGS), BF16),
            pltpu.SemaphoreType.DMA,
            pltpu.SemaphoreType.DMA((chunks,)),
        ],
        input_output_aliases=aliases,
        compiler_params=pltpu.CompilerParams(vmem_limit_bytes=VMEM_BYTES),
        cost_estimate=pl.CostEstimate(
            flops=4 * CH * CH * LAGS * depth, bytes_accessed=2 * CH * CH * LAGS, transcendentals=0
        ),
        name=f"lags_{slot}",
    )(*operands)


def body(strain, tile_pairs, tile_count):
    blocks = strain.shape[0] // CH
    wins = strain.shape[1]
    size = lax.axis_size("tile")
    depth = wins * 2 * BAND
    scale = 1.0 / math.sqrt(wins * BAND)
    consts = [jnp.asarray(t) for t in (fold_table(wins), mean_table(), dft_tables())]
    tables = [jnp.asarray(t) for t in phase_tables(scale)]
    ahead2 = [(i, i - 2) for i in range(2, size)]
    behind2 = [(i, i + 2) for i in range(size - 2)]
    across = [(i, i - 1) for i in range(2, size, 2)]
    swap = [(i, i ^ 1) for i in range(size)]

    view = strain.reshape(blocks * CH, wins, WIN // 128, 128).transpose(0, 2, 1, 3)
    view = view.reshape(blocks * CH, 2, 2, ROWS, 128)
    want = lax.ppermute(tile_pairs, "tile", behind2)
    (w0,) = spectra(first_kernel, view, consts, 0, 1, [], [(CH, depth)], "spectrum_0")
    far0 = lax.ppermute(w0, "tile", ahead2)
    w1, everything = spectra(
        rest_kernel, view, consts, 1, blocks - 1, [w0], [(CH, depth), (blocks, CH, depth)], "spectrum_rest"
    )
    near1 = lax.ppermute(w1, "tile", across)
    other = lax.ppermute(everything, "tile", swap)
    far2 = lax.ppermute(pick(want, everything, other), "tile", ahead2)
    out = None
    for slot, far in enumerate((far0, near1, far2)):
        out = corr_tile(
            slot, scale, tile_pairs, tile_count, tables, everything, other, far, out
        )
    return out


def solution(mesh):
    in_specs = (
        P(("groups", "tile"), None, None),
        P(("groups", "tile"), None),
        P(("groups", "tile")),
    )
    out_specs = P(("groups", "tile"), None, None)
    return jax.shard_map(body, mesh=mesh, in_specs=in_specs, out_specs=out_specs, check_vma=False)
```

```python
import functools
import math

import jax
import jax.numpy as jnp
import numpy as np
from jax import lax
from jax.experimental import pallas as pl
from jax.experimental.pallas import tpu as pltpu
from jax.sharding import PartitionSpec as P

CH = 128
WIN = 4096
BAND = 256
BIN0 = 60
SMOOTH = 64
LAGS = 64
ROWS = 16
BF16 = jnp.bfloat16
F32 = jnp.float32


def bin_order():
    return np.concatenate([np.arange(0, BAND, 2), np.arange(1, BAND, 2)])


def dft_tables():
    times = np.arange(WIN // 2, dtype=np.int64)[:, None]
    tables = []
    for parity in range(2):
        freqs = BIN0 + np.arange(parity, BAND, 2, dtype=np.int64)[None, :]
        angle = (times * freqs % WIN) * (2.0 * math.pi / WIN)
        tables.append(np.concatenate([np.cos(angle), -np.sin(angle)], 1))
    return np.stack(tables).astype(BF16)


def mean_table():
    group = bin_order() // SMOOTH
    return ((group[:, None] == group[None, :]) / SMOOTH).astype(BF16)


def phase_tables(coarse, scale):
    fine = LAGS // coarse
    freqs = (BIN0 + bin_order())[None, :]
    lags_a = fine * np.arange(1, coarse // 2 + 1)[:, None]
    lags_b = np.arange(fine)[:, None]
    step = 2.0 * math.pi / WIN
    a = np.concatenate([np.cos(lags_a * freqs * step), np.sin(lags_a * freqs * step)], 1) * scale
    b = np.concatenate([np.cos(lags_b * freqs * step), np.sin(lags_b * freqs * step)], 1)
    return a.astype(np.float32), b.astype(np.float32)


def spectra_kernel(wins, x_ref, mean_ref, tab_ref, w0_ref, w1_ref, all_ref, rows, left, acc):
    m, block = pl.program_id(0), pl.program_id(1)
    for half in range(2):
        rows[half] = x_ref[:, half, 0].reshape(CH * ROWS, 128).astype(F32)
    for s in range(ROWS // wins):
        for w in range(wins):
            first = rows[0, pl.ds(s * wins + w, CH, stride=ROWS), :]
            second = rows[1, pl.ds(s * wins + w, CH, stride=ROWS), :]
            place = (slice(w * CH, (w + 1) * CH), slice(s * 128, (s + 1) * 128))
            left[0, place[0], place[1]] = (first + second).astype(BF16)
            left[1, place[0], place[1]] = (first - second).astype(BF16)
    parts = [
        jnp.dot(left[sign], tab_ref[sign], preferred_element_type=F32) for sign in range(2)
    ]

    @pl.when(m == 0)
    def _():
        for sign in range(2):
            acc[block, sign] = parts[sign]

    @pl.when(m == 1)
    def _():
        spec = [acc[block, sign] + parts[sign] for sign in range(2)]
        energy = [s[:, :128] * s[:, :128] + s[:, 128:] * s[:, 128:] for s in spec]
        energy = jnp.concatenate(energy, 1)
        high = energy.astype(BF16)
        low = (energy - high.astype(F32)).astype(BF16)
        power = jnp.dot(high, mean_ref[...], preferred_element_type=F32)
        power += jnp.dot(low, mean_ref[...], preferred_element_type=F32)
        factor = lax.rsqrt(power + 1e-06)
        for w in range(wins):
            r = slice(w * CH, (w + 1) * CH)
            for q in range(4):
                sign, part = q % 2, q // 2
                value = spec[sign][r, part * 128 : (part + 1) * 128]
                value = value * factor[r, sign * 128 : (sign + 1) * 128]
                column = (w * 4 + q) * 128
                all_ref[block, :, column : column + 128] = value.astype(BF16)

        @pl.when(block == 0)
        def _():
            w0_ref[...] = all_ref[0]

        @pl.when(block == 1)
        def _():
            w1_ref[...] = all_ref[1]


def spectra(view, mean, table, blocks, wins):
    width = WIN // 4
    depth = wins * 2 * BAND
    shapes = [(CH, depth), (CH, depth), (blocks, CH, depth)]
    return pl.pallas_call(
        functools.partial(spectra_kernel, wins),
        grid=(2, blocks),
        out_shape=[jax.ShapeDtypeStruct(shape, BF16) for shape in shapes],
        in_specs=[
            pl.BlockSpec((CH, 2, 1, ROWS, 128), lambda m, b: (b, 0, m, 0, 0)),
            pl.BlockSpec((BAND, BAND), lambda m, b: (0, 0)),
            pl.BlockSpec((2, width, BAND), lambda m, b: (0, m, 0)),
        ],
        out_specs=[pl.BlockSpec(memory_space=pltpu.VMEM)] * len(shapes),
        scratch_shapes=[
            pltpu.VMEM((2, CH * ROWS, 128), F32),
            pltpu.VMEM((2, CH * wins, width), BF16),
            pltpu.VMEM((blocks, 2, CH * wins, BAND), F32),
        ],
        compiler_params=pltpu.CompilerParams(vmem_limit_bytes=60 * 2**20),
        cost_estimate=pl.CostEstimate(
            flops=2 * blocks * CH * wins * WIN * BAND,
            bytes_accessed=2 * blocks * CH * wins * WIN + 2 * WIN * BAND,
            transcendentals=0,
        ),
        name="spectra",
    )(view, mean, table)


def chosen(want, everything, other):
    blocks = everything.shape[0]
    me = lax.axis_index("tile")
    index = want - me * blocks
    own = lax.dynamic_index_in_dim(everything, jnp.clip(index, 0, blocks - 1), 0, keepdims=False)
    beside = lax.dynamic_index_in_dim(
        other, jnp.clip(index + blocks, 0, blocks - 1), 0, keepdims=False
    )
    return jnp.where(jnp.logical_or(index >= 0, me % 2 == 0), own, beside)


def corr_kernel(slot, blocks, scale, coarse, kind, *refs):
    pairs_ref, count_ref, row_ref, atab_ref, btab_ref, all_ref, other_ref, far_ref = refs[:8]
    out_hbm, raw, col, acoef, b0, b1, p0, p1, obuf, in_sem, out_sem = refs[-11:]
    fine = LAGS // coarse
    js = 256 // fine
    chunks = CH // js
    live = count_ref[0] > slot
    me = lax.axis_index("tile")
    index = pairs_ref[slot, 1] - me * blocks
    even = me % 2 == 0
    own = index < blocks
    beside = jnp.logical_and(index >= blocks, jnp.logical_and(even, index < 2 * blocks))
    remote = jnp.logical_not(jnp.logical_or(own, beside))

    def out_copy(c):
        columns = pl.ds(c * js * LAGS, js * LAGS)
        return pltpu.make_async_copy(
            obuf.at[:, columns], out_hbm.at[slot, :, columns], out_sem.at[c]
        )

    @pl.when(live)
    def _():
        @pl.when(own)
        def _():
            pltpu.make_async_copy(all_ref.at[jnp.clip(index, 0, blocks - 1)], raw, in_sem).start()

        @pl.when(beside)
        def _():
            pltpu.make_async_copy(
                other_ref.at[jnp.clip(index - blocks, 0, blocks - 1)], raw, in_sem
            ).start()

        @pl.when(remote)
        def _():
            pltpu.make_async_copy(far_ref, raw, in_sem).start()

        for w in range(2):
            for p in range(2):
                re_cols = slice((w * 4 + p) * 128, (w * 4 + p + 1) * 128)
                im_cols = slice((w * 4 + 2 + p) * 128, (w * 4 + 3 + p) * 128)
                re = row_ref[0, :, re_cols].astype(F32)
                im = row_ref[0, :, im_cols].astype(F32)

                def put(a, re_value, im_value):
                    rows = slice(a * CH, (a + 1) * CH)
                    acoef[rows, re_cols] = re_value.astype(BF16)
                    acoef[rows, im_cols] = im_value.astype(BF16)

                middle = coarse // 2
                put(middle, re * scale, im * scale)
                for n in range(1, middle + 1):
                    cos = atab_ref[n - 1 : n, p * 128 : (p + 1) * 128]
                    sin = atab_ref[n - 1 : n, (2 + p) * 128 : (3 + p) * 128]
                    rc, ic, rs, ims = re * cos, im * cos, re * sin, im * sin
                    put(middle - n, rc + ims, ic - rs)
                    if n < middle:
                        put(middle + n, rc - ims, ic + rs)
        pltpu.make_async_copy(far_ref, raw, in_sem).wait()
        for q in range(8):
            col[q] = raw[:, q * 128 : (q + 1) * 128].astype(F32)

        def build(c, b):
            for w in range(2):
                for p in range(2):
                    re_q, im_q = w * 4 + p, w * 4 + 2 + p
                    cos = btab_ref[:, p * 128 : (p + 1) * 128]
                    sin = btab_ref[:, (2 + p) * 128 : (3 + p) * 128]
                    step = max(ROWS // fine, 1)
                    for place in range(0, js, step):
                        res, ims = [], []
                        for pos in range(place, place + step):
                            v, inner = divmod(pos, 2 * coarse)
                            jj, q = divmod(inner, coarse)
                            j = c * js + v * 2 * coarse + 2 * q + jj
                            re = jnp.concatenate([col[re_q, pl.ds(j, 8, stride=0), :]] * (fine // 8), 0)
                            im = jnp.concatenate([col[im_q, pl.ds(j, 8, stride=0), :]] * (fine // 8), 0)
                            res.append(re * cos + im * sin)
                            ims.append(im * cos - re * sin)
                        rows = slice(place * fine, (place + step) * fine)
                        b[rows, re_q * 128 : (re_q + 1) * 128] = jnp.concatenate(res, 0).astype(BF16)
                        b[rows, im_q * 128 : (im_q + 1) * 128] = jnp.concatenate(ims, 0).astype(BF16)

        def multiply(b, p):
            p[...] = lax.dot_general(
                acoef[...], b[...], (((1,), (1,)), ((), ())), preferred_element_type=F32
            ).astype(kind)

        lane = lax.broadcasted_iota(jnp.int32, (CH, 128), 1)

        def arrange(c, prod):
            for v in range(2):
                x = [prod[a * CH : (a + 1) * CH, v * 128 : (v + 1) * 128] for a in range(coarse)]
                bit = 1
                while bit < coarse:
                    upper = (lane // fine) & bit != 0
                    for a in range(coarse):
                        if a & bit == 0:
                            lo, hi = x[a], x[a | bit]
                            x[a] = jnp.where(upper, pltpu.roll(hi, fine * bit, 1), lo)
                            x[a | bit] = jnp.where(upper, hi, pltpu.roll(lo, 128 - fine * bit, 1))
                    bit *= 2
                for q in range(coarse):
                    column = c * js * LAGS + (v * coarse + q) * 128
                    obuf[:, column : column + 128] = x[q].astype(BF16)
            out_copy(c).start()

        bs, ps = (b0, b1), (p0, p1)
        build(0, b0)
        for c in range(chunks):
            multiply(bs[c % 2], ps[c % 2])
            if c + 1 < chunks:
                build(c + 1, bs[(c + 1) % 2])
            if c > 0:
                arrange(c - 1, ps[(c - 1) % 2])
        arrange(chunks - 1, ps[(chunks - 1) % 2])

    @pl.when(jnp.logical_not(live))
    def _():
        obuf[...] = jnp.zeros_like(obuf)
        for c in range(chunks):
            out_copy(c).start()

    for c in range(chunks):
        out_copy(c).wait()


def corr_tile(slot, scale, coarse, kind, pairs, count, everything, other, far, buffer):
    fine = LAGS // coarse
    tables = [jnp.asarray(t) for t in phase_tables(coarse, scale)]
    js = 256 // fine
    chunks = CH // js
    blocks, _, depth = everything.shape
    in_specs = [
        pl.BlockSpec(memory_space=pltpu.SMEM),
        pl.BlockSpec(memory_space=pltpu.SMEM),
        pl.BlockSpec((1, CH, depth), lambda i: (slot, 0, 0)),
        pl.BlockSpec(memory_space=pltpu.VMEM),
        pl.BlockSpec(memory_space=pltpu.VMEM),
    ] + [pl.BlockSpec(memory_space=pl.ANY)] * 3
    operands = [pairs, count, everything, *tables, everything, other, far]
    aliases = {}
    if buffer is not None:
        aliases = {len(operands): 0}
        operands.append(buffer)
        in_specs.append(pl.BlockSpec(memory_space=pl.ANY))
    return pl.pallas_call(
        functools.partial(corr_kernel, slot, blocks, scale, coarse, kind),
        grid=(1,),
        out_shape=jax.ShapeDtypeStruct((blocks, CH, CH * LAGS), BF16),
        in_specs=in_specs,
        out_specs=pl.BlockSpec(memory_space=pl.ANY),
        scratch_shapes=[
            pltpu.VMEM((CH, depth), BF16),
            pltpu.VMEM((8, CH, 128), F32),
            pltpu.VMEM((coarse * CH, depth), BF16),
            pltpu.VMEM((js * fine, depth), BF16),
            pltpu.VMEM((js * fine, depth), BF16),
            pltpu.VMEM((coarse * CH, js * fine), kind),
            pltpu.VMEM((coarse * CH, js * fine), kind),
            pltpu.VMEM((CH, CH * LAGS), BF16),
            pltpu.SemaphoreType.DMA,
            pltpu.SemaphoreType.DMA((chunks,)),
        ],
        input_output_aliases=aliases,
        compiler_params=pltpu.CompilerParams(vmem_limit_bytes=24 * 2**20),
        cost_estimate=pl.CostEstimate(
            flops=4 * CH * CH * LAGS * depth, bytes_accessed=2 * CH * CH * LAGS, transcendentals=0
        ),
        name=f"lags_{slot}",
    )(*operands)


def body(strain, tile_pairs, tile_count):
    blocks = strain.shape[0] // CH
    wins = strain.shape[1]
    size = lax.axis_size("tile")
    depth = wins * 2 * BAND
    scale = 1.0 / math.sqrt(wins * BAND)
    mean, table = jnp.asarray(mean_table()), jnp.asarray(dft_tables())
    me = lax.axis_index("tile")
    ahead2 = [(i, i - 2) for i in range(2, size)]
    across = [(i, i - 1) for i in range(2, size, 2)]
    swap = [(i, i ^ 1) for i in range(size)]

    view = strain.reshape(blocks * CH, wins, WIN // 128, 128).transpose(0, 2, 1, 3)
    view = view.reshape(blocks * CH, 2, 2, ROWS, 128)
    wants = lax.all_gather(tile_pairs, "tile", tiled=True)
    want = lax.dynamic_index_in_dim(
        wants, jnp.maximum((me - 1) * blocks - 1, 0), 0, keepdims=False
    )[1]
    w0, w1, everything = spectra(view, mean, table, blocks, wins)
    far0 = lax.ppermute(w0, "tile", ahead2)
    near1 = lax.ppermute(w1, "tile", across)
    other = lax.ppermute(everything, "tile", swap)
    far2 = lax.ppermute(chosen(want, everything, other), "tile", ahead2)
    out = None
    forms = ((4, BF16), (2, BF16), (8, F32))
    for slot, far in enumerate((far0, near1, far2)):
        out = corr_tile(
            slot, scale, *forms[slot], tile_pairs, tile_count, everything, other, far, out
        )
    return out


def solution(mesh):
    in_specs = (
        P(("groups", "tile"), None, None),
        P(("groups", "tile"), None),
        P(("groups", "tile")),
    )
    out_specs = P(("groups", "tile"), None, None)
    return jax.shard_map(body, mesh=mesh, in_specs=in_specs, out_specs=out_specs, check_vma=False)
```

```python
import functools
import math

import jax
import jax.numpy as jnp
import numpy as np
from jax import lax
from jax.experimental import pallas as pl
from jax.experimental.pallas import tpu as pltpu
from jax.sharding import PartitionSpec as P

CH = 128
WIN = 4096
BAND = 256
BIN0 = 60
SMOOTH = 64
LAGS = 64
ROWS = 16
TOGETHER = 8
BF16 = jnp.bfloat16
F32 = jnp.float32


def bin_order():
    return np.concatenate([np.arange(0, BAND, 2), np.arange(1, BAND, 2)])


def dft_tables():
    times = np.arange(WIN // 2, dtype=np.int64)[:, None]
    tables = []
    for parity in range(2):
        freqs = BIN0 + np.arange(parity, BAND, 2, dtype=np.int64)[None, :]
        angle = (times * freqs % WIN) * (2.0 * math.pi / WIN)
        tables.append(np.concatenate([np.cos(angle), -np.sin(angle)], 1))
    return np.stack(tables).astype(BF16)


def mean_table():
    group = bin_order() // SMOOTH
    return ((group[:, None] == group[None, :]) / SMOOTH).astype(BF16)


def phase_tables(coarse, scale):
    fine = LAGS // coarse
    freqs = (BIN0 + bin_order())[None, :]
    lags_a = fine * np.arange(1, coarse // 2 + 1)[:, None]
    lags_b = np.arange(fine)[:, None]
    step = 2.0 * math.pi / WIN
    a = np.concatenate([np.cos(lags_a * freqs * step), np.sin(lags_a * freqs * step)], 1) * scale
    b = np.concatenate([np.cos(lags_b * freqs * step), np.sin(lags_b * freqs * step)], 1)
    return a.astype(np.float32), b.astype(np.float32)


def fold_table(wins):
    inner = ROWS // wins
    sign, s, w, c = np.unravel_index(np.arange(256), (2, inner, wins, TOGETHER))
    table = np.zeros((256, 256), np.float32)
    for half in range(2):
        column = np.ravel_multi_index((c, half + 0 * c, s, w), (TOGETHER, 2, inner, wins))
        table[np.arange(256), column] = np.where((sign == 1) & (half == 1), -1.0, 1.0)
    return table.astype(BF16)


def spectra_kernel(wins, x_ref, fold_ref, mean_ref, tab_hbm, w0_ref, w1_ref, all_ref, tab, left, sem):
    block, side = pl.program_id(0), pl.program_id(1)
    part = CH // 2
    start = jnp.logical_and(block == 0, side == 0)

    @pl.when(start)
    def _():
        pltpu.make_async_copy(tab_hbm, tab, sem).start()

    for m in range(2):
        for first in range(0, part // TOGETHER, 4):
            groups = []
            for g in range(first, first + 4):
                rows = x_ref[g * TOGETHER : (g + 1) * TOGETHER, :, m]
                groups.append(rows.reshape(TOGETHER * 2 * ROWS, 128))
            folded = jnp.dot(
                fold_ref[...], jnp.concatenate(groups, 1), preferred_element_type=F32
            )
            for sign in range(2):
                for s in range(ROWS // wins):
                    for w in range(wins):
                        row = ((sign * (ROWS // wins) + s) * wins + w) * TOGETHER
                        for n in range(0, 4, 2):
                            pair = [
                                folded[row : row + TOGETHER, k * 128 : (k + 1) * 128]
                                for k in (n, n + 1)
                            ]
                            to = w * part + (first + n) * TOGETHER
                            column = (m * (ROWS // wins) + s) * 128
                            left[sign, side, to : to + 2 * TOGETHER, column : column + 128] = (
                                jnp.concatenate(pair, 0).astype(BF16)
                            )

    @pl.when(jnp.logical_and(block == 0, side == 1))
    def _():
        pltpu.make_async_copy(tab_hbm, tab, sem).wait()

    @pl.when(side == 1)
    def _():
        spec = [
            jnp.dot(
                left[sign].reshape(CH * wins, WIN // 2), tab[sign], preferred_element_type=F32
            )
            for sign in range(2)
        ]
        energy = [s[:, :128] * s[:, :128] + s[:, 128:] * s[:, 128:] for s in spec]
        energy = jnp.concatenate(energy, 1)
        high = energy.astype(BF16)
        low = (energy - high.astype(F32)).astype(BF16)
        power = jnp.dot(high, mean_ref[...], preferred_element_type=F32)
        power += jnp.dot(low, mean_ref[...], preferred_element_type=F32)
        factor = lax.rsqrt(power + 1e-06)
        for h in range(2):
            for w in range(wins):
                r = slice((h * wins + w) * part, (h * wins + w + 1) * part)
                for q in range(4):
                    sign, half = q % 2, q // 2
                    value = spec[sign][r, half * 128 : (half + 1) * 128]
                    value = value * factor[r, sign * 128 : (sign + 1) * 128]
                    column = (w * 4 + q) * 128
                    all_ref[block, h * part : (h + 1) * part, column : column + 128] = (
                        value.astype(BF16)
                    )

        @pl.when(block == 0)
        def _():
            w0_ref[...] = all_ref[0]

        @pl.when(block == 1)
        def _():
            w1_ref[...] = all_ref[1]


def spectra(view, fold, mean, table, blocks, wins):
    depth = wins * 2 * BAND
    shapes = [(CH, depth), (CH, depth), (blocks, CH, depth)]
    return pl.pallas_call(
        functools.partial(spectra_kernel, wins),
        grid=(blocks, 2),
        out_shape=[jax.ShapeDtypeStruct(shape, BF16) for shape in shapes],
        in_specs=[
            pl.BlockSpec((CH // 2, 2, 2, ROWS, 128), lambda b, h: (2 * b + h, 0, 0, 0, 0)),
            pl.BlockSpec((256, 256), lambda b, h: (0, 0)),
            pl.BlockSpec((BAND, BAND), lambda b, h: (0, 0)),
            pl.BlockSpec(memory_space=pl.ANY),
        ],
        out_specs=[pl.BlockSpec(memory_space=pltpu.VMEM)] * len(shapes),
        scratch_shapes=[
            pltpu.VMEM((2, WIN // 2, BAND), BF16),
            pltpu.VMEM((2, 2, CH // 2 * wins, WIN // 2), BF16),
            pltpu.SemaphoreType.DMA,
        ],
        compiler_params=pltpu.CompilerParams(vmem_limit_bytes=60 * 2**20),
        cost_estimate=pl.CostEstimate(
            flops=2 * blocks * CH * wins * WIN * BAND,
            bytes_accessed=2 * blocks * CH * wins * WIN + 2 * WIN * BAND,
            transcendentals=0,
        ),
        name="spectra",
    )(view, fold, mean, table)


def chosen(want, everything, other):
    blocks = everything.shape[0]
    me = lax.axis_index("tile")
    index = want - me * blocks
    own = lax.dynamic_index_in_dim(everything, jnp.clip(index, 0, blocks - 1), 0, keepdims=False)
    beside = lax.dynamic_index_in_dim(
        other, jnp.clip(index + blocks, 0, blocks - 1), 0, keepdims=False
    )
    return jnp.where(jnp.logical_or(index >= 0, me % 2 == 0), own, beside)


def corr_kernel(slot, blocks, scale, coarse, kind, *refs):
    pairs_ref, count_ref, row_ref, atab_ref, btab_ref, all_ref, other_ref, far_ref = refs[:8]
    out_hbm, raw, col, acoef, b0, b1, p0, p1, obuf, in_sem, out_sem = refs[-11:]
    fine = LAGS // coarse
    js = 256 // fine
    chunks = CH // js
    live = count_ref[0] > slot
    me = lax.axis_index("tile")
    index = pairs_ref[slot, 1] - me * blocks
    even = me % 2 == 0
    own = index < blocks
    beside = jnp.logical_and(index >= blocks, jnp.logical_and(even, index < 2 * blocks))
    remote = jnp.logical_not(jnp.logical_or(own, beside))

    def out_copy(c):
        columns = pl.ds(c * js * LAGS, js * LAGS)
        return pltpu.make_async_copy(
            obuf.at[:, columns], out_hbm.at[slot, :, columns], out_sem.at[c]
        )

    @pl.when(live)
    def _():
        @pl.when(own)
        def _():
            pltpu.make_async_copy(all_ref.at[jnp.clip(index, 0, blocks - 1)], raw, in_sem).start()

        @pl.when(beside)
        def _():
            pltpu.make_async_copy(
                other_ref.at[jnp.clip(index - blocks, 0, blocks - 1)], raw, in_sem
            ).start()

        @pl.when(remote)
        def _():
            pltpu.make_async_copy(far_ref, raw, in_sem).start()

        for w in range(2):
            for p in range(2):
                re_cols = slice((w * 4 + p) * 128, (w * 4 + p + 1) * 128)
                im_cols = slice((w * 4 + 2 + p) * 128, (w * 4 + 3 + p) * 128)
                re = row_ref[0, :, re_cols].astype(F32)
                im = row_ref[0, :, im_cols].astype(F32)

                def put(a, re_value, im_value):
                    rows = slice(a * CH, (a + 1) * CH)
                    acoef[rows, re_cols] = re_value.astype(BF16)
                    acoef[rows, im_cols] = im_value.astype(BF16)

                middle = coarse // 2
                put(middle, re * scale, im * scale)
                for n in range(1, middle + 1):
                    cos = atab_ref[n - 1 : n, p * 128 : (p + 1) * 128]
                    sin = atab_ref[n - 1 : n, (2 + p) * 128 : (3 + p) * 128]
                    rc, ic, rs, ims = re * cos, im * cos, re * sin, im * sin
                    put(middle - n, rc + ims, ic - rs)
                    if n < middle:
                        put(middle + n, rc - ims, ic + rs)
        pltpu.make_async_copy(far_ref, raw, in_sem).wait()
        for q in range(8):
            col[q] = raw[:, q * 128 : (q + 1) * 128].astype(F32)

        def build(c, b):
            for w in range(2):
                for p in range(2):
                    re_q, im_q = w * 4 + p, w * 4 + 2 + p
                    cos = btab_ref[:, p * 128 : (p + 1) * 128]
                    sin = btab_ref[:, (2 + p) * 128 : (3 + p) * 128]
                    step = max(ROWS // fine, 1)
                    for place in range(0, js, step):
                        res, ims = [], []
                        for pos in range(place, place + step):
                            v, inner = divmod(pos, 2 * coarse)
                            jj, q = divmod(inner, coarse)
                            j = c * js + v * 2 * coarse + 2 * q + jj
                            re = jnp.concatenate([col[re_q, pl.ds(j, 8, stride=0), :]] * (fine // 8), 0)
                            im = jnp.concatenate([col[im_q, pl.ds(j, 8, stride=0), :]] * (fine // 8), 0)
                            res.append(re * cos + im * sin)
                            ims.append(im * cos - re * sin)
                        rows = slice(place * fine, (place + step) * fine)
                        b[rows, re_q * 128 : (re_q + 1) * 128] = jnp.concatenate(res, 0).astype(BF16)
                        b[rows, im_q * 128 : (im_q + 1) * 128] = jnp.concatenate(ims, 0).astype(BF16)

        def multiply(b, p):
            p[...] = lax.dot_general(
                acoef[...], b[...], (((1,), (1,)), ((), ())), preferred_element_type=F32
            ).astype(kind)

        lane = lax.broadcasted_iota(jnp.int32, (CH, 128), 1)

        def arrange(c, prod):
            for v in range(2):
                x = [prod[a * CH : (a + 1) * CH, v * 128 : (v + 1) * 128] for a in range(coarse)]
                bit = 1
                while bit < coarse:
                    upper = (lane // fine) & bit != 0
                    for a in range(coarse):
                        if a & bit == 0:
                            lo, hi = x[a], x[a | bit]
                            x[a] = jnp.where(upper, pltpu.roll(hi, fine * bit, 1), lo)
                            x[a | bit] = jnp.where(upper, hi, pltpu.roll(lo, 128 - fine * bit, 1))
                    bit *= 2
                for q in range(coarse):
                    column = c * js * LAGS + (v * coarse + q) * 128
                    obuf[:, column : column + 128] = x[q].astype(BF16)
            out_copy(c).start()

        bs, ps = (b0, b1), (p0, p1)
        build(0, b0)
        for c in range(chunks):
            multiply(bs[c % 2], ps[c % 2])
            if c > 0:
                arrange(c - 1, ps[(c - 1) % 2])
            if c + 1 < chunks:
                build(c + 1, bs[(c + 1) % 2])
        arrange(chunks - 1, ps[(chunks - 1) % 2])

    @pl.when(jnp.logical_not(live))
    def _():
        obuf[...] = jnp.zeros_like(obuf)
        for c in range(chunks):
            out_copy(c).start()

    for c in range(chunks):
        out_copy(c).wait()


def corr_tile(slot, scale, coarse, kind, pairs, count, everything, other, far, buffer):
    fine = LAGS // coarse
    tables = [jnp.asarray(t) for t in phase_tables(coarse, scale)]
    js = 256 // fine
    chunks = CH // js
    blocks, _, depth = everything.shape
    in_specs = [
        pl.BlockSpec(memory_space=pltpu.SMEM),
        pl.BlockSpec(memory_space=pltpu.SMEM),
        pl.BlockSpec((1, CH, depth), lambda i: (slot, 0, 0)),
        pl.BlockSpec(memory_space=pltpu.VMEM),
        pl.BlockSpec(memory_space=pltpu.VMEM),
    ] + [pl.BlockSpec(memory_space=pl.ANY)] * 3
    operands = [pairs, count, everything, *tables, everything, other, far]
    aliases = {}
    if buffer is not None:
        aliases = {len(operands): 0}
        operands.append(buffer)
        in_specs.append(pl.BlockSpec(memory_space=pl.ANY))
    return pl.pallas_call(
        functools.partial(corr_kernel, slot, blocks, scale, coarse, kind),
        grid=(1,),
        out_shape=jax.ShapeDtypeStruct((blocks, CH, CH * LAGS), BF16),
        in_specs=in_specs,
        out_specs=pl.BlockSpec(memory_space=pl.ANY),
        scratch_shapes=[
            pltpu.VMEM((CH, depth), BF16),
            pltpu.VMEM((8, CH, 128), F32),
            pltpu.VMEM((coarse * CH, depth), BF16),
            pltpu.VMEM((js * fine, depth), BF16),
            pltpu.VMEM((js * fine, depth), BF16),
            pltpu.VMEM((coarse * CH, js * fine), kind),
            pltpu.VMEM((coarse * CH, js * fine), kind),
            pltpu.VMEM((CH, CH * LAGS), BF16),
            pltpu.SemaphoreType.DMA,
            pltpu.SemaphoreType.DMA((chunks,)),
        ],
        input_output_aliases=aliases,
        compiler_params=pltpu.CompilerParams(vmem_limit_bytes=24 * 2**20),
        cost_estimate=pl.CostEstimate(
            flops=4 * CH * CH * LAGS * depth, bytes_accessed=2 * CH * CH * LAGS, transcendentals=0
        ),
        name=f"lags_{slot}",
    )(*operands)


def body(strain, tile_pairs, tile_count):
    blocks = strain.shape[0] // CH
    wins = strain.shape[1]
    size = lax.axis_size("tile")
    depth = wins * 2 * BAND
    scale = 1.0 / math.sqrt(wins * BAND)
    fold, mean, table = [jnp.asarray(t) for t in (fold_table(wins), mean_table(), dft_tables())]
    ahead2 = [(i, i - 2) for i in range(2, size)]
    across = [(i, i - 1) for i in range(2, size, 2)]
    swap = [(i, i ^ 1) for i in range(size)]

    view = strain.reshape(blocks * CH, wins, WIN // 128, 128).transpose(0, 2, 1, 3)
    view = view.reshape(blocks * CH, 2, 2, ROWS, 128)
    want = lax.ppermute(tile_pairs, "tile", [(i, i + 2) for i in range(size - 2)])
    w0, w1, everything = spectra(view, fold, mean, table, blocks, wins)
    far0 = lax.ppermute(w0, "tile", ahead2)
    near1 = lax.ppermute(w1, "tile", across)
    other = lax.ppermute(everything, "tile", swap)
    far2 = lax.ppermute(chosen(want[blocks - 1, 1], everything, other), "tile", ahead2)
    out = None
    forms = ((4, F32), (8, F32), (4, F32))
    for slot, far in enumerate((far0, near1, far2)):
        out = corr_tile(
            slot, scale, *forms[slot], tile_pairs, tile_count, everything, other, far, out
        )
    return out


def solution(mesh):
    in_specs = (
        P(("groups", "tile"), None, None),
        P(("groups", "tile"), None),
        P(("groups", "tile")),
    )
    out_specs = P(("groups", "tile"), None, None)
    return jax.shard_map(body, mesh=mesh, in_specs=in_specs, out_specs=out_specs, check_vma=False)
```

```python
import functools
import math

import jax
import jax.numpy as jnp
import numpy as np
from jax import lax
from jax.experimental import pallas as pl
from jax.experimental.pallas import tpu as pltpu
from jax.sharding import PartitionSpec as P

CH = 128
WIN = 4096
BAND = 256
BIN0 = 60
SMOOTH = 64
LAGS = 64
ROWS = 16
PITCH = 72
BF16 = jnp.bfloat16
F32 = jnp.float32


def bin_order():
    return np.concatenate([np.arange(0, BAND, 2), np.arange(1, BAND, 2)])


def dft_tables():
    times = np.arange(WIN // 2, dtype=np.int64)[:, None]
    tables = []
    for parity in range(2):
        freqs = BIN0 + np.arange(parity, BAND, 2, dtype=np.int64)[None, :]
        angle = (times * freqs % WIN) * (2.0 * math.pi / WIN)
        tables.append(np.concatenate([np.cos(angle), -np.sin(angle)], 1))
    group = bin_order() // SMOOTH
    tables.append((group[:, None] == group[None, :]) / SMOOTH)
    return np.concatenate(tables, 0).astype(BF16)


def phase_tables(coarse, scale):
    fine = LAGS // coarse
    freqs = (BIN0 + bin_order())[None, :]
    lags_a = fine * np.arange(1, coarse // 2 + 1)[:, None]
    lags_b = np.arange(fine)[:, None]
    step = 2.0 * math.pi / WIN
    a = np.concatenate([np.cos(lags_a * freqs * step), np.sin(lags_a * freqs * step)], 1) * scale
    b = np.concatenate([np.cos(lags_b * freqs * step), np.sin(lags_b * freqs * step)], 1)
    return a.astype(np.float32), b.astype(np.float32)


def spectra_kernel(blocks, wins, x_hbm, tab_hbm, w0_ref, w1_ref, all_ref, x, tab, rows, left, x_sem, t_sem):
    part = CH // 2
    half = WIN // 2
    per = WIN // 128 * wins

    def x_copy(n):
        channels = pl.ds(n * part, part)
        return pltpu.make_async_copy(x_hbm.at[channels], x.at[channels], x_sem.at[n])

    t_copy = pltpu.make_async_copy(tab_hbm, tab, t_sem)
    x_copy(0).start()
    x_copy(1).start()
    t_copy.start()
    for n in range(2, 2 * blocks):
        x_copy(n).start()

    def fold(b):
        for c in range(CH):
            rows[c * PITCH : c * PITCH + per, :] = x[b * CH + c].astype(F32)
        for t in range(half // 128):
            for w in range(wins):
                row = t * wins + w
                first = rows[pl.ds(row, CH, stride=PITCH), :]
                second = rows[pl.ds(row + per // 2, CH, stride=PITCH), :]
                place = (slice(w * CH, (w + 1) * CH), slice(t * 128, (t + 1) * 128))
                left[2 * b, place[0], place[1]] = (first + second).astype(BF16)
                left[2 * b + 1, place[0], place[1]] = (first - second).astype(BF16)

    def finish(b):
        spec = [
            jnp.dot(
                left[2 * b + sign],
                tab[sign * half : (sign + 1) * half, :],
                preferred_element_type=F32,
            )
            for sign in range(2)
        ]
        mean = tab[2 * half :, :]
        energy = [s[:, :128] * s[:, :128] + s[:, 128:] * s[:, 128:] for s in spec]
        energy = jnp.concatenate(energy, 1)
        high = energy.astype(BF16)
        low = (energy - high.astype(F32)).astype(BF16)
        power = jnp.dot(high, mean, preferred_element_type=F32)
        power += jnp.dot(low, mean, preferred_element_type=F32)
        factor = lax.rsqrt(power + 1e-06)
        for w in range(wins):
            r = slice(w * CH, (w + 1) * CH)
            for q in range(4):
                sign, side = q % 2, q // 2
                value = spec[sign][r, side * 128 : (side + 1) * 128]
                value = (value * factor[r, sign * 128 : (sign + 1) * 128]).astype(BF16)
                column = (w * 4 + q) * 128
                all_ref[b, :, column : column + 128] = value
                if b < 2:
                    (w0_ref, w1_ref)[b][:, column : column + 128] = value

    for b in range(blocks):
        x_copy(2 * b).wait()
        x_copy(2 * b + 1).wait()
        if b == 1:
            t_copy.wait()
        if b > 0:
            finish(b - 1)
        fold(b)
    finish(blocks - 1)


def spectra(view, table, blocks, wins):
    depth = wins * 2 * BAND
    shapes = [(CH, depth), (CH, depth), (blocks, CH, depth)]
    return pl.pallas_call(
        functools.partial(spectra_kernel, blocks, wins),
        out_shape=[jax.ShapeDtypeStruct(shape, BF16) for shape in shapes],
        in_specs=[pl.BlockSpec(memory_space=pl.ANY)] * 2,
        out_specs=[pl.BlockSpec(memory_space=pltpu.VMEM)] * len(shapes),
        scratch_shapes=[
            pltpu.VMEM(view.shape, BF16),
            pltpu.VMEM(table.shape, BF16),
            pltpu.VMEM((CH * PITCH, 128), F32),
            pltpu.VMEM((2 * blocks, CH * wins, WIN // 2), BF16),
            pltpu.SemaphoreType.DMA((2 * blocks,)),
            pltpu.SemaphoreType.DMA,
        ],
        compiler_params=pltpu.CompilerParams(vmem_limit_bytes=52 * 2**20),
        cost_estimate=pl.CostEstimate(
            flops=2 * blocks * CH * wins * WIN * BAND,
            bytes_accessed=2 * blocks * CH * wins * WIN + 2 * WIN * BAND,
            transcendentals=0,
        ),
        name="spectra",
    )(view, table)


def chosen(want, everything, other):
    blocks = everything.shape[0]
    me = lax.axis_index("tile")
    index = want - me * blocks
    own = lax.dynamic_index_in_dim(everything, jnp.clip(index, 0, blocks - 1), 0, keepdims=False)
    beside = lax.dynamic_index_in_dim(
        other, jnp.clip(index + blocks, 0, blocks - 1), 0, keepdims=False
    )
    return jnp.where(jnp.logical_or(index >= 0, me % 2 == 0), own, beside)


def corr_kernel(slots, blocks, scale, coarse, *refs):
    fine = LAGS // coarse
    js = 256 // fine
    chunks = CH // js
    count = len(slots)
    pairs_ref, count_ref, atab_ref, btab_ref, all_ref, other_ref = refs[:6]
    fars = refs[6 : 6 + count]
    row_refs = refs[6 + count : 6 + 2 * count]
    out_hbm, raw, col, acoef, b0, b1, p0, p1, obuf, in_sem, out_sem = refs[-11:]
    me = lax.axis_index("tile")
    even = me % 2 == 0

    def out_copy(n, c):
        columns = pl.ds(c * js * LAGS, js * LAGS)
        return pltpu.make_async_copy(
            obuf.at[n, :, columns], out_hbm.at[slots[n], :, columns], out_sem.at[n, c]
        )

    def fetch(n):
        index = pairs_ref[slots[n], 1] - me * blocks
        own = index < blocks
        beside = jnp.logical_and(index >= blocks, jnp.logical_and(even, index < 2 * blocks))
        remote = jnp.logical_not(jnp.logical_or(own, beside))

        @pl.when(own)
        def _():
            source = all_ref.at[jnp.clip(index, 0, blocks - 1)]
            pltpu.make_async_copy(source, raw.at[n], in_sem.at[n]).start()

        @pl.when(beside)
        def _():
            source = other_ref.at[jnp.clip(index - blocks, 0, blocks - 1)]
            pltpu.make_async_copy(source, raw.at[n], in_sem.at[n]).start()

        @pl.when(remote)
        def _():
            pltpu.make_async_copy(fars[n], raw.at[n], in_sem.at[n]).start()

    def prepare(n):
        live = jnp.where(count_ref[0] > slots[n], 1.0, 0.0).astype(F32)
        for w in range(2):
            for p in range(2):
                re_cols = slice((w * 4 + p) * 128, (w * 4 + p + 1) * 128)
                im_cols = slice((w * 4 + 2 + p) * 128, (w * 4 + 3 + p) * 128)
                re = row_refs[n][0, :, re_cols].astype(F32)
                im = row_refs[n][0, :, im_cols].astype(F32)

                def put(a, re_value, im_value):
                    rows = slice(a * CH, (a + 1) * CH)
                    acoef[n, rows, re_cols] = re_value.astype(BF16)
                    acoef[n, rows, im_cols] = im_value.astype(BF16)

                middle = coarse // 2
                put(middle, re * (scale * live), im * (scale * live))
                for k in range(1, middle + 1):
                    cos = atab_ref[k - 1 : k, p * 128 : (p + 1) * 128] * live
                    sin = atab_ref[k - 1 : k, (2 + p) * 128 : (3 + p) * 128] * live
                    rc, ic, rs, ims = re * cos, im * cos, re * sin, im * sin
                    put(middle - k, rc + ims, ic - rs)
                    if k < middle:
                        put(middle + k, rc - ims, ic + rs)

    def build(n, c, b):
        for w in range(2):
            for p in range(2):
                re_q, im_q = w * 4 + p, w * 4 + 2 + p
                cos = btab_ref[:, p * 128 : (p + 1) * 128]
                sin = btab_ref[:, (2 + p) * 128 : (3 + p) * 128]
                step = max(ROWS // fine, 1)
                for place in range(0, js, step):
                    res, ims = [], []
                    for pos in range(place, place + step):
                        v, inner = divmod(pos, 2 * coarse)
                        jj, q = divmod(inner, coarse)
                        j = c * js + v * 2 * coarse + 2 * q + jj
                        re = col[n, re_q, pl.ds(j, 8, stride=0), :]
                        im = col[n, im_q, pl.ds(j, 8, stride=0), :]
                        re = jnp.concatenate([re] * (fine // 8), 0)
                        im = jnp.concatenate([im] * (fine // 8), 0)
                        res.append(re * cos + im * sin)
                        ims.append(im * cos - re * sin)
                    rows = slice(place * fine, (place + step) * fine)
                    b[rows, re_q * 128 : (re_q + 1) * 128] = jnp.concatenate(res, 0).astype(BF16)
                    b[rows, im_q * 128 : (im_q + 1) * 128] = jnp.concatenate(ims, 0).astype(BF16)

    def multiply(n, b, p):
        p[...] = lax.dot_general(
            acoef[n], b[...], (((1,), (1,)), ((), ())), preferred_element_type=F32
        )

    lane = lax.broadcasted_iota(jnp.int32, (CH, 128), 1)

    def arrange(n, c, prod):
        for v in range(2):
            x = [prod[a * CH : (a + 1) * CH, v * 128 : (v + 1) * 128] for a in range(coarse)]
            bit = 1
            while bit < coarse:
                upper = (lane // fine) & bit != 0
                for a in range(coarse):
                    if a & bit == 0:
                        lo, hi = x[a], x[a | bit]
                        x[a] = jnp.where(upper, pltpu.roll(hi, fine * bit, 1), lo)
                        x[a | bit] = jnp.where(upper, hi, pltpu.roll(lo, 128 - fine * bit, 1))
                bit *= 2
            for q in range(coarse):
                column = c * js * LAGS + (v * coarse + q) * 128
                obuf[n, :, column : column + 128] = x[q].astype(BF16)
        out_copy(n, c).start()

    def run():
        for n in range(count):
            fetch(n)
        prepare(0)
        for n in range(count):
            pltpu.make_async_copy(fars[n], raw.at[n], in_sem.at[n]).wait()
        bs, ps = (b0, b1), (p0, p1)
        steps = [(n, c) for n in range(count) for c in range(chunks)]

        def ready(k):
            n, c = steps[k]
            if c == 0:
                if n > 0:
                    prepare(n)
                for q in range(8):
                    col[n, q] = raw[n, :, q * 128 : (q + 1) * 128].astype(F32)
            build(n, c, bs[k % 2])

        ready(0)
        for k, (n, c) in enumerate(steps):
            multiply(n, bs[k % 2], ps[k % 2])
            if k > 0:
                arrange(*steps[k - 1], ps[(k - 1) % 2])
            if k + 1 < len(steps):
                ready(k + 1)
        arrange(*steps[-1], ps[(len(steps) - 1) % 2])

    if count == 1:
        live = count_ref[0] > slots[0]
        pl.when(live)(run)

        @pl.when(jnp.logical_not(live))
        def _():
            obuf[...] = jnp.zeros_like(obuf)
            for c in range(chunks):
                out_copy(0, c).start()
    else:
        run()
    for n in range(count):
        for c in range(chunks):
            out_copy(n, c).wait()


def corr_tiles(slots, scale, coarse, pairs, tile_count, everything, other, fars, buffer):
    fine = LAGS // coarse
    tables = [jnp.asarray(t) for t in phase_tables(coarse, scale)]
    js = 256 // fine
    chunks = CH // js
    count = len(slots)
    blocks, _, depth = everything.shape
    in_specs = [
        pl.BlockSpec(memory_space=pltpu.SMEM),
        pl.BlockSpec(memory_space=pltpu.SMEM),
        pl.BlockSpec(memory_space=pltpu.VMEM),
        pl.BlockSpec(memory_space=pltpu.VMEM),
    ] + [pl.BlockSpec(memory_space=pl.ANY)] * (2 + count)
    in_specs += [pl.BlockSpec((1, CH, depth), lambda i, s=s: (s, 0, 0)) for s in slots]
    operands = [pairs, tile_count, *tables, everything, other, *fars] + [everything] * count
    aliases = {}
    if buffer is not None:
        aliases = {len(operands): 0}
        operands.append(buffer)
        in_specs.append(pl.BlockSpec(memory_space=pl.ANY))
    return pl.pallas_call(
        functools.partial(corr_kernel, slots, blocks, scale, coarse),
        grid=(1,),
        out_shape=jax.ShapeDtypeStruct((blocks, CH, CH * LAGS), BF16),
        in_specs=in_specs,
        out_specs=pl.BlockSpec(memory_space=pl.ANY),
        scratch_shapes=[
            pltpu.VMEM((count, CH, depth), BF16),
            pltpu.VMEM((count, 8, CH, 128), F32),
            pltpu.VMEM((count, coarse * CH, depth), BF16),
            pltpu.VMEM((js * fine, depth), BF16),
            pltpu.VMEM((js * fine, depth), BF16),
            pltpu.VMEM((coarse * CH, js * fine), F32),
            pltpu.VMEM((coarse * CH, js * fine), F32),
            pltpu.VMEM((count, CH, CH * LAGS), BF16),
            pltpu.SemaphoreType.DMA((count,)),
            pltpu.SemaphoreType.DMA((count, chunks)),
        ],
        input_output_aliases=aliases,
        compiler_params=pltpu.CompilerParams(vmem_limit_bytes=32 * 2**20),
        cost_estimate=pl.CostEstimate(
            flops=4 * count * CH * CH * LAGS * depth,
            bytes_accessed=2 * count * CH * CH * LAGS,
            transcendentals=0,
        ),
        name="lags_" + "_".join(str(s) for s in slots),
    )(*operands)


def body(strain, tile_pairs, tile_count):
    blocks = strain.shape[0] // CH
    wins = strain.shape[1]
    size = lax.axis_size("tile")
    depth = wins * 2 * BAND
    scale = 1.0 / math.sqrt(wins * BAND)
    table = jnp.asarray(dft_tables())
    ahead2 = [(i, i - 2) for i in range(2, size)]
    behind2 = [(i, i + 2) for i in range(size - 2)]
    across = [(i, i - 1) for i in range(2, size, 2)]
    swap = [(i, i ^ 1) for i in range(size)]

    view = strain.reshape(blocks * CH, wins, WIN // 128, 128).transpose(0, 2, 1, 3)
    view = view.reshape(blocks * CH, WIN // 128 * wins, 128)
    want = lax.ppermute(tile_pairs, "tile", behind2)[blocks - 1, 1]
    w0, w1, everything = spectra(view, table, blocks, wins)
    far0 = lax.ppermute(w0, "tile", ahead2)
    near1 = lax.ppermute(w1, "tile", across)
    other = lax.ppermute(everything, "tile", swap)
    far2 = lax.ppermute(chosen(want, everything, other), "tile", ahead2)
    shared = (scale, 8, tile_pairs, tile_count, everything, other)
    out = corr_tiles((0, 1), *shared, (far0, near1), None)
    return corr_tiles((2,), *shared, (far2,), out)


def solution(mesh):
    in_specs = (
        P(("groups", "tile"), None, None),
        P(("groups", "tile"), None),
        P(("groups", "tile")),
    )
    out_specs = P(("groups", "tile"), None, None)
    return jax.shard_map(body, mesh=mesh, in_specs=in_specs, out_specs=out_specs, check_vma=False)
```

```python
import functools
import math

import jax
import jax.numpy as jnp
import numpy as np
from jax import lax
from jax.experimental import pallas as pl
from jax.experimental.pallas import tpu as pltpu
from jax.sharding import PartitionSpec as P

CH = 128
WIN = 4096
BAND = 256
BIN0 = 60
SMOOTH = 64
LAGS = 64
ROWS = 16
PITCH = 72
BF16 = jnp.bfloat16
F32 = jnp.float32


def bin_order():
    return np.concatenate([np.arange(0, BAND, 2), np.arange(1, BAND, 2)])


def dft_tables():
    times = np.arange(WIN // 2, dtype=np.int64)[:, None]
    tables = []
    for parity in range(2):
        freqs = BIN0 + np.arange(parity, BAND, 2, dtype=np.int64)[None, :]
        angle = (times * freqs % WIN) * (2.0 * math.pi / WIN)
        tables.append(np.concatenate([np.cos(angle), -np.sin(angle)], 1))
    group = bin_order() // SMOOTH
    tables.append((group[:, None] == group[None, :]) / SMOOTH)
    return np.concatenate(tables, 0).astype(BF16)


def phase_tables(coarse, scale):
    fine = LAGS // coarse
    freqs = (BIN0 + bin_order())[None, :]
    lags_a = fine * np.arange(1, coarse // 2 + 1)[:, None]
    lags_b = np.arange(fine)[:, None]
    step = 2.0 * math.pi / WIN
    a = np.concatenate([np.cos(lags_a * freqs * step), np.sin(lags_a * freqs * step)], 1) * scale
    b = np.concatenate([np.cos(lags_b * freqs * step), np.sin(lags_b * freqs * step)], 1)
    return a.astype(np.float32), b.astype(np.float32)


def spectra_kernel(
    blocks, wins, want_ref, x_hbm, tab_hbm, w0_ref, w1_ref, all_ref, own_ref, x, tab, rows, left, x_sem, t_sem
):
    part = CH // 2
    half = WIN // 2
    per = WIN // 128 * wins

    def x_copy(n):
        channels = pl.ds(n * part, part)
        return pltpu.make_async_copy(x_hbm.at[channels], x.at[channels], x_sem.at[n])

    t_copy = pltpu.make_async_copy(tab_hbm, tab, t_sem)
    x_copy(0).start()
    x_copy(1).start()
    t_copy.start()
    for n in range(2, 2 * blocks):
        x_copy(n).start()

    def fold(b):
        for c in range(CH):
            rows[c * PITCH : c * PITCH + per, :] = x[b * CH + c].astype(F32)
        for t in range(half // 128):
            for w in range(wins):
                row = t * wins + w
                first = rows[pl.ds(row, CH, stride=PITCH), :]
                second = rows[pl.ds(row + per // 2, CH, stride=PITCH), :]
                place = (slice(w * CH, (w + 1) * CH), slice(t * 128, (t + 1) * 128))
                left[2 * b, place[0], place[1]] = (first + second).astype(BF16)
                left[2 * b + 1, place[0], place[1]] = (first - second).astype(BF16)

    def finish(b):
        spec = [
            jnp.dot(
                left[2 * b + sign],
                tab[sign * half : (sign + 1) * half, :],
                preferred_element_type=F32,
            )
            for sign in range(2)
        ]
        mean = tab[2 * half :, :]
        energy = [s[:, :128] * s[:, :128] + s[:, 128:] * s[:, 128:] for s in spec]
        energy = jnp.concatenate(energy, 1)
        high = energy.astype(BF16)
        low = (energy - high.astype(F32)).astype(BF16)
        power = jnp.dot(high, mean, preferred_element_type=F32)
        power += jnp.dot(low, mean, preferred_element_type=F32)
        factor = lax.rsqrt(power + 1e-06)
        for w in range(wins):
            r = slice(w * CH, (w + 1) * CH)
            for q in range(4):
                sign, side = q % 2, q // 2
                value = spec[sign][r, side * 128 : (side + 1) * 128]
                value = (value * factor[r, sign * 128 : (sign + 1) * 128]).astype(BF16)
                column = (w * 4 + q) * 128
                all_ref[b, :, column : column + 128] = value
                if b < 2:
                    (w0_ref, w1_ref)[b][:, column : column + 128] = value

    for b in range(blocks):
        x_copy(2 * b).wait()
        x_copy(2 * b + 1).wait()
        if b == 1:
            t_copy.wait()
        if b > 0:
            finish(b - 1)
        fold(b)
    finish(blocks - 1)
    index = want_ref[blocks - 1, 1] - lax.axis_index("tile") * blocks
    own_ref[...] = all_ref[jnp.clip(index, 0, blocks - 1)]


def spectra(want, view, table, blocks, wins):
    depth = wins * 2 * BAND
    shapes = [(CH, depth), (CH, depth), (blocks, CH, depth), (CH, depth)]
    return pl.pallas_call(
        functools.partial(spectra_kernel, blocks, wins),
        out_shape=[jax.ShapeDtypeStruct(shape, BF16) for shape in shapes],
        in_specs=[pl.BlockSpec(memory_space=pltpu.SMEM)] + [pl.BlockSpec(memory_space=pl.ANY)] * 2,
        out_specs=[pl.BlockSpec(memory_space=pltpu.VMEM)] * len(shapes),
        scratch_shapes=[
            pltpu.VMEM(view.shape, BF16),
            pltpu.VMEM(table.shape, BF16),
            pltpu.VMEM((CH * PITCH, 128), F32),
            pltpu.VMEM((2 * blocks, CH * wins, WIN // 2), BF16),
            pltpu.SemaphoreType.DMA((2 * blocks,)),
            pltpu.SemaphoreType.DMA,
        ],
        compiler_params=pltpu.CompilerParams(vmem_limit_bytes=52 * 2**20),
        cost_estimate=pl.CostEstimate(
            flops=2 * blocks * CH * wins * WIN * BAND,
            bytes_accessed=2 * blocks * CH * wins * WIN + 2 * WIN * BAND,
            transcendentals=0,
        ),
        name="spectra",
    )(want, view, table)


def chosen(want, blocks, own, other):
    me = lax.axis_index("tile")
    index = want[blocks - 1 :, 1:] - me * blocks
    beside = other[blocks - 1]
    for k in range(blocks - 1):
        beside = jnp.where(index + blocks == k, other[k], beside)
    return jnp.where(jnp.logical_or(index >= 0, me % 2 == 0), own, beside)


def corr_kernel(slots, blocks, scale, coarse, *refs):
    fine = LAGS // coarse
    js = 256 // fine
    chunks = CH // js
    count = len(slots)
    pairs_ref, count_ref, atab_ref, btab_ref, all_ref, other_ref = refs[:6]
    fars = refs[6 : 6 + count]
    row_refs = refs[6 + count : 6 + 2 * count]
    out_hbm, raw, col, acoef, b0, b1, p0, p1, obuf, in_sem, out_sem = refs[-11:]
    me = lax.axis_index("tile")
    even = me % 2 == 0

    def out_copy(n, c):
        columns = pl.ds(c * js * LAGS, js * LAGS)
        return pltpu.make_async_copy(
            obuf.at[n, :, columns], out_hbm.at[slots[n], :, columns], out_sem.at[n, c]
        )

    def fetch(n):
        index = pairs_ref[slots[n], 1] - me * blocks
        own = index < blocks
        beside = jnp.logical_and(index >= blocks, jnp.logical_and(even, index < 2 * blocks))
        remote = jnp.logical_not(jnp.logical_or(own, beside))

        @pl.when(own)
        def _():
            source = all_ref.at[jnp.clip(index, 0, blocks - 1)]
            pltpu.make_async_copy(source, raw.at[n], in_sem.at[n]).start()

        @pl.when(beside)
        def _():
            source = other_ref.at[jnp.clip(index - blocks, 0, blocks - 1)]
            pltpu.make_async_copy(source, raw.at[n], in_sem.at[n]).start()

        @pl.when(remote)
        def _():
            pltpu.make_async_copy(fars[n], raw.at[n], in_sem.at[n]).start()

    def prepare(n):
        live = jnp.where(count_ref[0] > slots[n], 1.0, 0.0).astype(F32)
        for w in range(2):
            for p in range(2):
                re_cols = slice((w * 4 + p) * 128, (w * 4 + p + 1) * 128)
                im_cols = slice((w * 4 + 2 + p) * 128, (w * 4 + 3 + p) * 128)
                re = row_refs[n][0, :, re_cols].astype(F32)
                im = row_refs[n][0, :, im_cols].astype(F32)

                def put(a, re_value, im_value):
                    rows = slice(a * CH, (a + 1) * CH)
                    acoef[n, rows, re_cols] = re_value.astype(BF16)
                    acoef[n, rows, im_cols] = im_value.astype(BF16)

                middle = coarse // 2
                put(middle, re * (scale * live), im * (scale * live))
                for k in range(1, middle + 1):
                    cos = atab_ref[k - 1 : k, p * 128 : (p + 1) * 128] * live
                    sin = atab_ref[k - 1 : k, (2 + p) * 128 : (3 + p) * 128] * live
                    rc, ic, rs, ims = re * cos, im * cos, re * sin, im * sin
                    put(middle - k, rc + ims, ic - rs)
                    if k < middle:
                        put(middle + k, rc - ims, ic + rs)

    def build(n, c, b):
        for w in range(2):
            for p in range(2):
                re_q, im_q = w * 4 + p, w * 4 + 2 + p
                cos = btab_ref[:, p * 128 : (p + 1) * 128]
                sin = btab_ref[:, (2 + p) * 128 : (3 + p) * 128]
                step = max(ROWS // fine, 1)
                for place in range(0, js, step):
                    res, ims = [], []
                    for pos in range(place, place + step):
                        v, inner = divmod(pos, 2 * coarse)
                        jj, q = divmod(inner, coarse)
                        j = c * js + v * 2 * coarse + 2 * q + jj
                        re = col[n, re_q, pl.ds(j, 8, stride=0), :]
                        im = col[n, im_q, pl.ds(j, 8, stride=0), :]
                        re = jnp.concatenate([re] * (fine // 8), 0)
                        im = jnp.concatenate([im] * (fine // 8), 0)
                        res.append(re * cos + im * sin)
                        ims.append(im * cos - re * sin)
                    rows = slice(place * fine, (place + step) * fine)
                    b[rows, re_q * 128 : (re_q + 1) * 128] = jnp.concatenate(res, 0).astype(BF16)
                    b[rows, im_q * 128 : (im_q + 1) * 128] = jnp.concatenate(ims, 0).astype(BF16)

    def multiply(n, b, p):
        p[...] = lax.dot_general(
            acoef[n], b[...], (((1,), (1,)), ((), ())), preferred_element_type=F32
        )

    lane = lax.broadcasted_iota(jnp.int32, (CH, 128), 1)

    def arrange(n, c, prod):
        for v in range(2):
            x = [prod[a * CH : (a + 1) * CH, v * 128 : (v + 1) * 128] for a in range(coarse)]
            bit = 1
            while bit < coarse:
                upper = (lane // fine) & bit != 0
                for a in range(coarse):
                    if a & bit == 0:
                        lo, hi = x[a], x[a | bit]
                        x[a] = jnp.where(upper, pltpu.roll(hi, fine * bit, 1), lo)
                        x[a | bit] = jnp.where(upper, hi, pltpu.roll(lo, 128 - fine * bit, 1))
                bit *= 2
            for q in range(coarse):
                column = c * js * LAGS + (v * coarse + q) * 128
                obuf[n, :, column : column + 128] = x[q].astype(BF16)
        out_copy(n, c).start()

    def run():
        for n in range(count):
            fetch(n)
        prepare(0)
        for n in range(count):
            pltpu.make_async_copy(fars[n], raw.at[n], in_sem.at[n]).wait()
        bs, ps = (b0, b1), (p0, p1)
        steps = [(n, c) for n in range(count) for c in range(chunks)]

        def ready(k):
            n, c = steps[k]
            if c == 0:
                if n > 0:
                    prepare(n)
                for q in range(8):
                    col[n, q] = raw[n, :, q * 128 : (q + 1) * 128].astype(F32)
            build(n, c, bs[k % 2])

        ready(0)
        for k, (n, c) in enumerate(steps):
            multiply(n, bs[k % 2], ps[k % 2])
            if k > 0:
                arrange(*steps[k - 1], ps[(k - 1) % 2])
            if k + 1 < len(steps):
                ready(k + 1)
        arrange(*steps[-1], ps[(len(steps) - 1) % 2])

    if count == 1:
        live = count_ref[0] > slots[0]
        pl.when(live)(run)

        @pl.when(jnp.logical_not(live))
        def _():
            obuf[...] = jnp.zeros_like(obuf)
            for c in range(chunks):
                out_copy(0, c).start()
    else:
        run()
    for n in range(count):
        for c in range(chunks):
            out_copy(n, c).wait()


def corr_tiles(slots, scale, coarse, pairs, tile_count, everything, other, fars, buffer):
    fine = LAGS // coarse
    tables = [jnp.asarray(t) for t in phase_tables(coarse, scale)]
    js = 256 // fine
    chunks = CH // js
    count = len(slots)
    blocks, _, depth = everything.shape
    in_specs = [
        pl.BlockSpec(memory_space=pltpu.SMEM),
        pl.BlockSpec(memory_space=pltpu.SMEM),
        pl.BlockSpec(memory_space=pltpu.VMEM),
        pl.BlockSpec(memory_space=pltpu.VMEM),
    ] + [pl.BlockSpec(memory_space=pl.ANY)] * (2 + count)
    in_specs += [pl.BlockSpec((1, CH, depth), lambda i, s=s: (s, 0, 0)) for s in slots]
    operands = [pairs, tile_count, *tables, everything, other, *fars] + [everything] * count
    aliases = {}
    if buffer is not None:
        aliases = {len(operands): 0}
        operands.append(buffer)
        in_specs.append(pl.BlockSpec(memory_space=pl.ANY))
    return pl.pallas_call(
        functools.partial(corr_kernel, slots, blocks, scale, coarse),
        grid=(1,),
        out_shape=jax.ShapeDtypeStruct((blocks, CH, CH * LAGS), BF16),
        in_specs=in_specs,
        out_specs=pl.BlockSpec(memory_space=pl.ANY),
        scratch_shapes=[
            pltpu.VMEM((count, CH, depth), BF16),
            pltpu.VMEM((count, 8, CH, 128), F32),
            pltpu.VMEM((count, coarse * CH, depth), BF16),
            pltpu.VMEM((js * fine, depth), BF16),
            pltpu.VMEM((js * fine, depth), BF16),
            pltpu.VMEM((coarse * CH, js * fine), F32),
            pltpu.VMEM((coarse * CH, js * fine), F32),
            pltpu.VMEM((count, CH, CH * LAGS), BF16),
            pltpu.SemaphoreType.DMA((count,)),
            pltpu.SemaphoreType.DMA((count, chunks)),
        ],
        input_output_aliases=aliases,
        compiler_params=pltpu.CompilerParams(vmem_limit_bytes=32 * 2**20),
        cost_estimate=pl.CostEstimate(
            flops=4 * count * CH * CH * LAGS * depth,
            bytes_accessed=2 * count * CH * CH * LAGS,
            transcendentals=0,
        ),
        name="lags_" + "_".join(str(s) for s in slots),
    )(*operands)


def body(strain, tile_pairs, tile_count):
    blocks = strain.shape[0] // CH
    wins = strain.shape[1]
    size = lax.axis_size("tile")
    depth = wins * 2 * BAND
    scale = 1.0 / math.sqrt(wins * BAND)
    table = jnp.asarray(dft_tables())
    ahead2 = [(i, i - 2) for i in range(2, size)]
    behind2 = [(i, i + 2) for i in range(size - 2)]
    across = [(i, i - 1) for i in range(2, size, 2)]
    swap = [(i, i ^ 1) for i in range(size)]

    view = strain.reshape(blocks * CH, wins, WIN // 128, 128).transpose(0, 2, 1, 3)
    view = view.reshape(blocks * CH, WIN // 128 * wins, 128)
    want = lax.ppermute(tile_pairs, "tile", behind2)
    w0, w1, everything, own = spectra(want, view, table, blocks, wins)
    far0 = lax.ppermute(w0, "tile", ahead2)
    near1 = lax.ppermute(w1, "tile", across)
    other = lax.ppermute(everything, "tile", swap)
    far2 = lax.ppermute(chosen(want, blocks, own, other), "tile", ahead2)
    shared = (scale, 4, tile_pairs, tile_count, everything, other)
    out = corr_tiles((0, 1), *shared, (far0, near1), None)
    return corr_tiles((2,), *shared, (far2,), out)


def solution(mesh):
    in_specs = (
        P(("groups", "tile"), None, None),
        P(("groups", "tile"), None),
        P(("groups", "tile")),
    )
    out_specs = P(("groups", "tile"), None, None)
    return jax.shard_map(body, mesh=mesh, in_specs=in_specs, out_specs=out_specs, check_vma=False)
```

```python
import functools
import math

import jax
import jax.numpy as jnp
import numpy as np
from jax import lax
from jax.experimental import pallas as pl
from jax.experimental.pallas import tpu as pltpu
from jax.sharding import PartitionSpec as P

CH = 128
WIN = 4096
BAND = 256
BIN0 = 60
SMOOTH = 64
LAGS = 64
ROWS = 16
PITCH = 72
BF16 = jnp.bfloat16
F32 = jnp.float32


def bin_order():
    return np.concatenate([np.arange(0, BAND, 2), np.arange(1, BAND, 2)])


def dft_tables():
    times = np.arange(WIN // 2, dtype=np.int64)[:, None]
    tables = []
    for parity in range(2):
        freqs = BIN0 + np.arange(parity, BAND, 2, dtype=np.int64)[None, :]
        angle = (times * freqs % WIN) * (2.0 * math.pi / WIN)
        tables.append(np.concatenate([np.cos(angle), -np.sin(angle)], 1))
    group = bin_order() // SMOOTH
    tables.append((group[:, None] == group[None, :]) / SMOOTH)
    return np.concatenate(tables, 0).astype(BF16)


def phase_tables(coarse, scale):
    fine = LAGS // coarse
    freqs = (BIN0 + bin_order())[None, :]
    lags_a = fine * np.arange(1, coarse // 2 + 1)[:, None]
    lags_b = np.arange(fine)[:, None]
    step = 2.0 * math.pi / WIN
    a = np.concatenate([np.cos(lags_a * freqs * step), np.sin(lags_a * freqs * step)], 1) * scale
    b = np.concatenate([np.cos(lags_b * freqs * step), np.sin(lags_b * freqs * step)], 1)
    return a.astype(np.float32), b.astype(np.float32)


def spectra_kernel(blocks, wins, x_hbm, tab_hbm, w0_ref, w1_ref, all_ref, x, tab, rows, left, x_sem, t_sem):
    part = CH // 2
    half = WIN // 2
    per = WIN // 128 * wins

    def x_copy(n):
        channels = pl.ds(n * part, part)
        return pltpu.make_async_copy(x_hbm.at[channels], x.at[channels], x_sem.at[n])

    t_copy = pltpu.make_async_copy(tab_hbm, tab, t_sem)
    x_copy(0).start()
    x_copy(1).start()
    t_copy.start()
    for n in range(2, 2 * blocks):
        x_copy(n).start()

    def fold(b):
        for c in range(CH):
            rows[c * PITCH : c * PITCH + per, :] = x[b * CH + c].astype(F32)
        for t in range(half // 128):
            for w in range(wins):
                row = t * wins + w
                first = rows[pl.ds(row, CH, stride=PITCH), :]
                second = rows[pl.ds(row + per // 2, CH, stride=PITCH), :]
                place = (slice(w * CH, (w + 1) * CH), slice(t * 128, (t + 1) * 128))
                left[2 * b, place[0], place[1]] = (first + second).astype(BF16)
                left[2 * b + 1, place[0], place[1]] = (first - second).astype(BF16)

    def finish(b):
        spec = [
            jnp.dot(
                left[2 * b + sign],
                tab[sign * half : (sign + 1) * half, :],
                preferred_element_type=F32,
            )
            for sign in range(2)
        ]
        mean = tab[2 * half :, :]
        energy = [s[:, :128] * s[:, :128] + s[:, 128:] * s[:, 128:] for s in spec]
        energy = jnp.concatenate(energy, 1)
        high = energy.astype(BF16)
        low = (energy - high.astype(F32)).astype(BF16)
        power = jnp.dot(high, mean, preferred_element_type=F32)
        power += jnp.dot(low, mean, preferred_element_type=F32)
        factor = lax.rsqrt(power + 1e-06)
        for w in range(wins):
            r = slice(w * CH, (w + 1) * CH)
            for q in range(4):
                sign, side = q % 2, q // 2
                value = spec[sign][r, side * 128 : (side + 1) * 128]
                value = (value * factor[r, sign * 128 : (sign + 1) * 128]).astype(BF16)
                column = (w * 4 + q) * 128
                all_ref[b, :, column : column + 128] = value
                if b < 2:
                    (w0_ref, w1_ref)[b][:, column : column + 128] = value

    for b in range(blocks):
        x_copy(2 * b).wait()
        x_copy(2 * b + 1).wait()
        if b == 1:
            t_copy.wait()
        if b > 0:
            finish(b - 1)
        fold(b)
    finish(blocks - 1)


def spectra(view, table, blocks, wins):
    depth = wins * 2 * BAND
    shapes = [(CH, depth), (CH, depth), (blocks, CH, depth)]
    return pl.pallas_call(
        functools.partial(spectra_kernel, blocks, wins),
        out_shape=[jax.ShapeDtypeStruct(shape, BF16) for shape in shapes],
        in_specs=[pl.BlockSpec(memory_space=pl.ANY)] * 2,
        out_specs=[pl.BlockSpec(memory_space=pltpu.VMEM)] * len(shapes),
        scratch_shapes=[
            pltpu.VMEM(view.shape, BF16),
            pltpu.VMEM(table.shape, BF16),
            pltpu.VMEM((CH * PITCH, 128), F32),
            pltpu.VMEM((2 * blocks, CH * wins, WIN // 2), BF16),
            pltpu.SemaphoreType.DMA((2 * blocks,)),
            pltpu.SemaphoreType.DMA,
        ],
        compiler_params=pltpu.CompilerParams(vmem_limit_bytes=52 * 2**20),
        cost_estimate=pl.CostEstimate(
            flops=2 * blocks * CH * wins * WIN * BAND,
            bytes_accessed=2 * blocks * CH * wins * WIN + 2 * WIN * BAND,
            transcendentals=0,
        ),
        name="spectra",
    )(view, table)


def corr_kernel(slot, blocks, scale, coarse, kinds, choose, *refs):
    fine = LAGS // coarse
    js = 256 // fine
    chunks = CH // js
    slots, count = (slot,), 1
    pairs_ref, count_ref, atab_ref, btab_ref, row_ref = refs[:5]
    sources = refs[5 : 5 + len(kinds)]
    out_hbm = refs[-12 if choose else -11]
    raw, col, acoef, b0, b1, p0, p1, obuf, in_sem, out_sem = refs[-10:]
    me = lax.axis_index("tile")
    even = me % 2 == 0

    def out_copy(n, c):
        columns = pl.ds(c * js * LAGS, js * LAGS)
        return pltpu.make_async_copy(
            obuf.at[n, :, columns], out_hbm.at[slots[n], :, columns], out_sem.at[n, c]
        )

    def fetch(n):
        index = pairs_ref[slot, 1] - me * blocks
        for source, (begin, length, who) in zip(sources, kinds):
            here = jnp.logical_and(index >= begin, index < begin + length)
            if who is not None:
                here = jnp.logical_and(here, even if who == 0 else jnp.logical_not(even))

            @pl.when(here)
            def _(source=source, begin=begin, length=length):
                if len(source.shape) == 3:
                    source = source.at[jnp.clip(index - begin, 0, length - 1)]
                pltpu.make_async_copy(source, raw.at[n], in_sem.at[n]).start()

    def prepare(n):
        live = jnp.where(count_ref[0] > slots[n], 1.0, 0.0).astype(F32)
        for w in range(2):
            for p in range(2):
                re_cols = slice((w * 4 + p) * 128, (w * 4 + p + 1) * 128)
                im_cols = slice((w * 4 + 2 + p) * 128, (w * 4 + 3 + p) * 128)
                re = row_ref[0, :, re_cols].astype(F32)
                im = row_ref[0, :, im_cols].astype(F32)

                def put(a, re_value, im_value):
                    rows = slice(a * CH, (a + 1) * CH)
                    acoef[n, rows, re_cols] = re_value.astype(BF16)
                    acoef[n, rows, im_cols] = im_value.astype(BF16)

                middle = coarse // 2
                put(middle, re * (scale * live), im * (scale * live))
                for k in range(1, middle + 1):
                    cos = atab_ref[k - 1 : k, p * 128 : (p + 1) * 128] * live
                    sin = atab_ref[k - 1 : k, (2 + p) * 128 : (3 + p) * 128] * live
                    rc, ic, rs, ims = re * cos, im * cos, re * sin, im * sin
                    put(middle - k, rc + ims, ic - rs)
                    if k < middle:
                        put(middle + k, rc - ims, ic + rs)

    def build(n, c, b):
        for w in range(2):
            for p in range(2):
                re_q, im_q = w * 4 + p, w * 4 + 2 + p
                cos = btab_ref[:, p * 128 : (p + 1) * 128]
                sin = btab_ref[:, (2 + p) * 128 : (3 + p) * 128]
                step = max(ROWS // fine, 1)
                for place in range(0, js, step):
                    res, ims = [], []
                    for pos in range(place, place + step):
                        v, inner = divmod(pos, 2 * coarse)
                        jj, q = divmod(inner, coarse)
                        j = c * js + v * 2 * coarse + 2 * q + jj
                        re = col[n, re_q, pl.ds(j, 8, stride=0), :]
                        im = col[n, im_q, pl.ds(j, 8, stride=0), :]
                        re = jnp.concatenate([re] * (fine // 8), 0)
                        im = jnp.concatenate([im] * (fine // 8), 0)
                        res.append(re * cos + im * sin)
                        ims.append(im * cos - re * sin)
                    rows = slice(place * fine, (place + step) * fine)
                    b[rows, re_q * 128 : (re_q + 1) * 128] = jnp.concatenate(res, 0).astype(BF16)
                    b[rows, im_q * 128 : (im_q + 1) * 128] = jnp.concatenate(ims, 0).astype(BF16)

    def multiply(n, b, p):
        p[...] = lax.dot_general(
            acoef[n], b[...], (((1,), (1,)), ((), ())), preferred_element_type=F32
        )

    lane = lax.broadcasted_iota(jnp.int32, (CH, 128), 1)

    def arrange(n, c, prod):
        for v in range(2):
            x = [prod[a * CH : (a + 1) * CH, v * 128 : (v + 1) * 128] for a in range(coarse)]
            bit = 1
            while bit < coarse:
                upper = (lane // fine) & bit != 0
                for a in range(coarse):
                    if a & bit == 0:
                        lo, hi = x[a], x[a | bit]
                        x[a] = jnp.where(upper, pltpu.roll(hi, fine * bit, 1), lo)
                        x[a | bit] = jnp.where(upper, hi, pltpu.roll(lo, 128 - fine * bit, 1))
                bit *= 2
            for q in range(coarse):
                column = c * js * LAGS + (v * coarse + q) * 128
                obuf[n, :, column : column + 128] = x[q].astype(BF16)
        out_copy(n, c).start()

    def run():
        for n in range(count):
            fetch(n)
        prepare(0)
        for n in range(count):
            pltpu.make_async_copy(raw.at[n], raw.at[n], in_sem.at[n]).wait()
        bs, ps = (b0, b1), (p0, p1)
        steps = [(n, c) for n in range(count) for c in range(chunks)]

        def ready(k):
            n, c = steps[k]
            if c == 0:
                if n > 0:
                    prepare(n)
                for q in range(8):
                    col[n, q] = raw[n, :, q * 128 : (q + 1) * 128].astype(F32)
            build(n, c, bs[k % 2])

        ready(0)
        for k, (n, c) in enumerate(steps):
            multiply(n, bs[k % 2], ps[k % 2])
            if k > 0:
                arrange(*steps[k - 1], ps[(k - 1) % 2])
            if k + 1 < len(steps):
                ready(k + 1)
        arrange(*steps[-1], ps[(len(steps) - 1) % 2])

    if choose:
        want = refs[5 + len(kinds)][blocks - 1, 1] - me * blocks
        here = jnp.logical_or(even, want >= 0)

        @pl.when(here)
        def _():
            source = sources[0].at[jnp.clip(want, 0, blocks - 1)]
            pltpu.make_async_copy(source, refs[-11], in_sem.at[1]).start()

        @pl.when(jnp.logical_not(here))
        def _():
            source = sources[1].at[jnp.clip(want + blocks, 0, blocks - 1)]
            pltpu.make_async_copy(source, refs[-11], in_sem.at[1]).start()

    live = count_ref[0] > slot
    pl.when(live)(run)

    @pl.when(jnp.logical_not(live))
    def _():
        obuf[...] = jnp.zeros_like(obuf)
        for c in range(chunks):
            out_copy(0, c).start()

    for c in range(chunks):
        out_copy(0, c).wait()
    if choose:
        pltpu.make_async_copy(refs[-11], refs[-11], in_sem.at[1]).wait()


def corr_tile(slot, scale, coarse, pairs, tile_count, everything, sources, want, buffer):
    fine = LAGS // coarse
    tables = [jnp.asarray(t) for t in phase_tables(coarse, scale)]
    js = 256 // fine
    chunks = CH // js
    blocks, _, depth = everything.shape
    choose = want is not None
    hbm = pl.BlockSpec(memory_space=pl.ANY)
    in_specs = [
        pl.BlockSpec(memory_space=pltpu.SMEM),
        pl.BlockSpec(memory_space=pltpu.SMEM),
        pl.BlockSpec(memory_space=pltpu.VMEM),
        pl.BlockSpec(memory_space=pltpu.VMEM),
        pl.BlockSpec((1, CH, depth), lambda i: (slot, 0, 0)),
    ] + [hbm] * len(sources)
    operands = [pairs, tile_count, *tables, everything, *[s[0] for s in sources]]
    if choose:
        operands.append(want)
        in_specs.append(pl.BlockSpec(memory_space=pltpu.SMEM))
    aliases = {}
    if buffer is not None:
        aliases = {len(operands): 0}
        operands.append(buffer)
        in_specs.append(hbm)
    outs = [jax.ShapeDtypeStruct((blocks, CH, CH * LAGS), BF16)]
    if choose:
        outs.append(jax.ShapeDtypeStruct((CH, depth), BF16))
    return pl.pallas_call(
        functools.partial(corr_kernel, slot, blocks, scale, coarse, [s[1:] for s in sources], choose),
        grid=(1,),
        out_shape=outs,
        in_specs=in_specs,
        out_specs=[hbm] * len(outs),
        scratch_shapes=[
            pltpu.VMEM((1, CH, depth), BF16),
            pltpu.VMEM((1, 8, CH, 128), F32),
            pltpu.VMEM((1, coarse * CH, depth), BF16),
            pltpu.VMEM((js * fine, depth), BF16),
            pltpu.VMEM((js * fine, depth), BF16),
            pltpu.VMEM((coarse * CH, js * fine), F32),
            pltpu.VMEM((coarse * CH, js * fine), F32),
            pltpu.VMEM((1, CH, CH * LAGS), BF16),
            pltpu.SemaphoreType.DMA((2,)),
            pltpu.SemaphoreType.DMA((1, chunks)),
        ],
        input_output_aliases=aliases,
        compiler_params=pltpu.CompilerParams(vmem_limit_bytes=32 * 2**20),
        cost_estimate=pl.CostEstimate(
            flops=4 * CH * CH * LAGS * depth,
            bytes_accessed=2 * CH * CH * LAGS,
            transcendentals=0,
        ),
        name=f"lags_{slot}",
    )(*operands)


def body(strain, tile_pairs, tile_count):
    blocks = strain.shape[0] // CH
    wins = strain.shape[1]
    size = lax.axis_size("tile")
    depth = wins * 2 * BAND
    scale = 1.0 / math.sqrt(wins * BAND)
    table = jnp.asarray(dft_tables())
    ahead2 = [(i, i - 2) for i in range(2, size)]
    behind2 = [(i, i + 2) for i in range(size - 2)]
    across = [(i, i - 1) for i in range(2, size, 2)]
    swap = [(i, i ^ 1) for i in range(size)]

    view = strain.reshape(blocks * CH, wins, WIN // 128, 128).transpose(0, 2, 1, 3)
    view = view.reshape(blocks * CH, WIN // 128 * wins, 128)
    want = lax.ppermute(tile_pairs, "tile", behind2)
    w0, w1, everything = spectra(view, table, blocks, wins)
    far0 = lax.ppermute(w0, "tile", ahead2)
    other = lax.ppermute(everything, "tile", swap)
    near1 = lax.ppermute(jnp.where(want[:1, :1] >= 0, w1, w0), "tile", across)
    shared = (scale, 4, tile_pairs, tile_count, everything)
    even, odd = 0, 1
    own = (everything, 0, blocks, None)
    beside = (other, blocks, blocks, even)
    out, block = corr_tile(0, *shared, [own, beside, (far0, 2 * blocks, 1, None)], want, None)
    far2 = lax.ppermute(block, "tile", ahead2)
    (out,) = corr_tile(1, *shared, [own, beside, (near1, blocks + 1, 1, odd)], None, out)
    chosen = [(far2, blocks, blocks, odd), (far2, 2 * blocks, blocks, None)]
    (out,) = corr_tile(2, *shared, [own, beside, *chosen], None, out)
    return out


def solution(mesh):
    in_specs = (
        P(("groups", "tile"), None, None),
        P(("groups", "tile"), None),
        P(("groups", "tile")),
    )
    out_specs = P(("groups", "tile"), None, None)
    return jax.shard_map(body, mesh=mesh, in_specs=in_specs, out_specs=out_specs, check_vma=False)
```

```python
import functools
import math

import jax
import jax.numpy as jnp
import numpy as np
from jax import lax
from jax.experimental import pallas as pl
from jax.experimental.pallas import tpu as pltpu
from jax.sharding import PartitionSpec as P

CH = 128
WIN = 4096
BAND = 256
BIN0 = 60
SMOOTH = 64
LAGS = 64
ROWS = 16
PITCH = 72
BF16 = jnp.bfloat16
F32 = jnp.float32


def bin_order():
    return np.concatenate([np.arange(0, BAND, 2), np.arange(1, BAND, 2)])


def dft_tables():
    times = np.arange(WIN // 2, dtype=np.int64)[:, None]
    tables = []
    for parity in range(2):
        freqs = BIN0 + np.arange(parity, BAND, 2, dtype=np.int64)[None, :]
        angle = (times * freqs % WIN) * (2.0 * math.pi / WIN)
        tables.append(np.concatenate([np.cos(angle), -np.sin(angle)], 1))
    group = bin_order() // SMOOTH
    tables.append((group[:, None] == group[None, :]) / SMOOTH)
    return np.concatenate(tables, 0).astype(BF16)


def phase_tables(coarse, scale):
    fine = LAGS // coarse
    freqs = (BIN0 + bin_order())[None, :]
    lags_a = fine * np.arange(1, coarse // 2 + 1)[:, None]
    lags_b = np.arange(fine)[:, None]
    step = 2.0 * math.pi / WIN
    a = np.concatenate([np.cos(lags_a * freqs * step), np.sin(lags_a * freqs * step)], 1) * scale
    b = np.concatenate([np.cos(lags_b * freqs * step), np.sin(lags_b * freqs * step)], 1)
    return a.astype(np.float32), b.astype(np.float32)


def spectra_kernel(blocks, wins, x_hbm, tab_hbm, w0_ref, w1_ref, all_ref, x, tab, rows, left, x_sem, t_sem):
    part = CH // 2
    half = WIN // 2
    per = WIN // 128 * wins

    def x_copy(n):
        channels = pl.ds(n * part, part)
        return pltpu.make_async_copy(x_hbm.at[channels], x.at[channels], x_sem.at[n])

    t_copy = pltpu.make_async_copy(tab_hbm, tab, t_sem)
    x_copy(0).start()
    x_copy(1).start()
    t_copy.start()
    for n in range(2, 2 * blocks):
        x_copy(n).start()

    def fold(b, side):
        first = side * part
        for c in range(first, first + part):
            rows[c * PITCH : c * PITCH + per, :] = x[b * CH + c].astype(F32)
        for t in range(half // 128):
            for w in range(wins):
                row = first * PITCH + t * wins + w
                head = rows[pl.ds(row, part, stride=PITCH), :]
                tail = rows[pl.ds(row + per // 2, part, stride=PITCH), :]
                place = (slice(w * CH + first, w * CH + first + part), slice(t * 128, (t + 1) * 128))
                left[2 * b, place[0], place[1]] = (head + tail).astype(BF16)
                left[2 * b + 1, place[0], place[1]] = (head - tail).astype(BF16)

    def finish(b):
        spec = [
            jnp.dot(
                left[2 * b + sign],
                tab[sign * half : (sign + 1) * half, :],
                preferred_element_type=F32,
            )
            for sign in range(2)
        ]
        mean = tab[2 * half :, :]
        energy = [s[:, :128] * s[:, :128] + s[:, 128:] * s[:, 128:] for s in spec]
        energy = jnp.concatenate(energy, 1)
        high = energy.astype(BF16)
        low = (energy - high.astype(F32)).astype(BF16)
        power = jnp.dot(high, mean, preferred_element_type=F32)
        power += jnp.dot(low, mean, preferred_element_type=F32)
        factor = lax.rsqrt(power + 1e-06)
        for w in range(wins):
            r = slice(w * CH, (w + 1) * CH)
            for q in range(4):
                sign, side = q % 2, q // 2
                value = spec[sign][r, side * 128 : (side + 1) * 128]
                value = (value * factor[r, sign * 128 : (sign + 1) * 128]).astype(BF16)
                column = (w * 4 + q) * 128
                all_ref[b, :, column : column + 128] = value
                if b < 2:
                    (w0_ref, w1_ref)[b][:, column : column + 128] = value

    x_copy(0).wait()
    fold(0, 0)
    x_copy(1).wait()
    fold(0, 1)
    t_copy.wait()
    for b in range(1, blocks):
        x_copy(2 * b).wait()
        x_copy(2 * b + 1).wait()
        finish(b - 1)
        fold(b, 0)
        fold(b, 1)
    finish(blocks - 1)


def spectra(view, table, blocks, wins):
    depth = wins * 2 * BAND
    shapes = [(CH, depth), (CH, depth), (blocks, CH, depth)]
    return pl.pallas_call(
        functools.partial(spectra_kernel, blocks, wins),
        out_shape=[jax.ShapeDtypeStruct(shape, BF16) for shape in shapes],
        in_specs=[pl.BlockSpec(memory_space=pl.ANY)] * 2,
        out_specs=[pl.BlockSpec(memory_space=pltpu.VMEM)] * len(shapes),
        scratch_shapes=[
            pltpu.VMEM(view.shape, BF16),
            pltpu.VMEM(table.shape, BF16),
            pltpu.VMEM((CH * PITCH, 128), F32),
            pltpu.VMEM((2 * blocks, CH * wins, WIN // 2), BF16),
            pltpu.SemaphoreType.DMA((2 * blocks,)),
            pltpu.SemaphoreType.DMA,
        ],
        compiler_params=pltpu.CompilerParams(vmem_limit_bytes=52 * 2**20),
        cost_estimate=pl.CostEstimate(
            flops=2 * blocks * CH * wins * WIN * BAND,
            bytes_accessed=2 * blocks * CH * wins * WIN + 2 * WIN * BAND,
            transcendentals=0,
        ),
        name="spectra",
    )(view, table)


def chosen(want, everything, other):
    blocks = everything.shape[0]
    me = lax.axis_index("tile")
    index = want - me * blocks
    own = lax.dynamic_index_in_dim(everything, jnp.clip(index, 0, blocks - 1), 0, keepdims=False)
    beside = lax.dynamic_index_in_dim(
        other, jnp.clip(index + blocks, 0, blocks - 1), 0, keepdims=False
    )
    return jnp.where(jnp.logical_or(index >= 0, me % 2 == 0), own, beside)


def corr_kernel(slots, blocks, scale, coarse, *refs):
    fine = LAGS // coarse
    js = 256 // fine
    chunks = CH // js
    count = len(slots)
    pairs_ref, count_ref, atab_ref, btab_ref, all_ref, other_ref = refs[:6]
    fars = refs[6 : 6 + count]
    row_refs = refs[6 + count : 6 + 2 * count]
    out_hbm, raw, col, acoef, b0, b1, p0, p1, obuf, in_sem, out_sem = refs[-11:]
    me = lax.axis_index("tile")
    even = me % 2 == 0

    def out_copy(n, c):
        columns = pl.ds(c * js * LAGS, js * LAGS)
        return pltpu.make_async_copy(
            obuf.at[n, :, columns], out_hbm.at[slots[n], :, columns], out_sem.at[n, c]
        )

    def fetch(n):
        index = pairs_ref[slots[n], 1] - me * blocks
        own = index < blocks
        beside = jnp.logical_and(index >= blocks, jnp.logical_and(even, index < 2 * blocks))
        remote = jnp.logical_not(jnp.logical_or(own, beside))

        @pl.when(own)
        def _():
            source = all_ref.at[jnp.clip(index, 0, blocks - 1)]
            pltpu.make_async_copy(source, raw.at[n], in_sem.at[n]).start()

        @pl.when(beside)
        def _():
            source = other_ref.at[jnp.clip(index - blocks, 0, blocks - 1)]
            pltpu.make_async_copy(source, raw.at[n], in_sem.at[n]).start()

        @pl.when(remote)
        def _():
            pltpu.make_async_copy(fars[n], raw.at[n], in_sem.at[n]).start()

    def prepare(n):
        live = jnp.where(count_ref[0] > slots[n], 1.0, 0.0).astype(F32)
        for w in range(2):
            for p in range(2):
                re_cols = slice((w * 4 + p) * 128, (w * 4 + p + 1) * 128)
                im_cols = slice((w * 4 + 2 + p) * 128, (w * 4 + 3 + p) * 128)
                re = row_refs[n][0, :, re_cols].astype(F32)
                im = row_refs[n][0, :, im_cols].astype(F32)

                def put(a, re_value, im_value):
                    rows = slice(a * CH, (a + 1) * CH)
                    acoef[n, rows, re_cols] = re_value.astype(BF16)
                    acoef[n, rows, im_cols] = im_value.astype(BF16)

                middle = coarse // 2
                put(middle, re * (scale * live), im * (scale * live))
                for k in range(1, middle + 1):
                    cos = atab_ref[k - 1 : k, p * 128 : (p + 1) * 128] * live
                    sin = atab_ref[k - 1 : k, (2 + p) * 128 : (3 + p) * 128] * live
                    rc, ic, rs, ims = re * cos, im * cos, re * sin, im * sin
                    put(middle - k, rc + ims, ic - rs)
                    if k < middle:
                        put(middle + k, rc - ims, ic + rs)

    def build(n, c, b):
        for w in range(2):
            for p in range(2):
                re_q, im_q = w * 4 + p, w * 4 + 2 + p
                cos = btab_ref[:, p * 128 : (p + 1) * 128]
                sin = btab_ref[:, (2 + p) * 128 : (3 + p) * 128]
                step = max(ROWS // fine, 1)
                for place in range(0, js, step):
                    res, ims = [], []
                    for pos in range(place, place + step):
                        v, inner = divmod(pos, 2 * coarse)
                        jj, q = divmod(inner, coarse)
                        j = c * js + v * 2 * coarse + 2 * q + jj
                        re = col[n, re_q, pl.ds(j, 8, stride=0), :]
                        im = col[n, im_q, pl.ds(j, 8, stride=0), :]
                        re = jnp.concatenate([re] * (fine // 8), 0)
                        im = jnp.concatenate([im] * (fine // 8), 0)
                        res.append(re * cos + im * sin)
                        ims.append(im * cos - re * sin)
                    rows = slice(place * fine, (place + step) * fine)
                    b[rows, re_q * 128 : (re_q + 1) * 128] = jnp.concatenate(res, 0).astype(BF16)
                    b[rows, im_q * 128 : (im_q + 1) * 128] = jnp.concatenate(ims, 0).astype(BF16)

    def multiply(n, b, p):
        p[...] = lax.dot_general(
            acoef[n], b[...], (((1,), (1,)), ((), ())), preferred_element_type=F32
        )

    lane = lax.broadcasted_iota(jnp.int32, (CH, 128), 1)

    def arrange(n, c, prod):
        for v in range(2):
            x = [prod[a * CH : (a + 1) * CH, v * 128 : (v + 1) * 128] for a in range(coarse)]
            bit = 1
            while bit < coarse:
                upper = (lane // fine) & bit != 0
                for a in range(coarse):
                    if a & bit == 0:
                        lo, hi = x[a], x[a | bit]
                        x[a] = jnp.where(upper, pltpu.roll(hi, fine * bit, 1), lo)
                        x[a | bit] = jnp.where(upper, hi, pltpu.roll(lo, 128 - fine * bit, 1))
                bit *= 2
            for q in range(coarse):
                column = c * js * LAGS + (v * coarse + q) * 128
                obuf[n, :, column : column + 128] = x[q].astype(BF16)
        out_copy(n, c).start()

    def run():
        for n in range(count):
            fetch(n)
        prepare(0)
        for n in range(count):
            pltpu.make_async_copy(fars[n], raw.at[n], in_sem.at[n]).wait()
        bs, ps = (b0, b1), (p0, p1)
        steps = [(n, c) for n in range(count) for c in range(chunks)]

        def ready(k):
            n, c = steps[k]
            if c == 0:
                if n > 0:
                    prepare(n)
                for q in range(8):
                    col[n, q] = raw[n, :, q * 128 : (q + 1) * 128].astype(F32)
            build(n, c, bs[k % 2])

        ready(0)
        for k, (n, c) in enumerate(steps):
            multiply(n, bs[k % 2], ps[k % 2])
            if k > 0:
                arrange(*steps[k - 1], ps[(k - 1) % 2])
            if k + 1 < len(steps):
                ready(k + 1)
        arrange(*steps[-1], ps[(len(steps) - 1) % 2])

    if count == 1:
        live = count_ref[0] > slots[0]
        pl.when(live)(run)

        @pl.when(jnp.logical_not(live))
        def _():
            obuf[...] = jnp.zeros_like(obuf)
            for c in range(chunks):
                out_copy(0, c).start()
    else:
        run()
    for n in range(count):
        for c in range(chunks):
            out_copy(n, c).wait()


def corr_tiles(slots, scale, coarse, pairs, tile_count, everything, other, fars, buffer):
    fine = LAGS // coarse
    tables = [jnp.asarray(t) for t in phase_tables(coarse, scale)]
    js = 256 // fine
    chunks = CH // js
    count = len(slots)
    blocks, _, depth = everything.shape
    in_specs = [
        pl.BlockSpec(memory_space=pltpu.SMEM),
        pl.BlockSpec(memory_space=pltpu.SMEM),
        pl.BlockSpec(memory_space=pltpu.VMEM),
        pl.BlockSpec(memory_space=pltpu.VMEM),
    ] + [pl.BlockSpec(memory_space=pl.ANY)] * (2 + count)
    in_specs += [pl.BlockSpec((1, CH, depth), lambda i, s=s: (s, 0, 0)) for s in slots]
    operands = [pairs, tile_count, *tables, everything, other, *fars] + [everything] * count
    aliases = {}
    if buffer is not None:
        aliases = {len(operands): 0}
        operands.append(buffer)
        in_specs.append(pl.BlockSpec(memory_space=pl.ANY))
    return pl.pallas_call(
        functools.partial(corr_kernel, slots, blocks, scale, coarse),
        grid=(1,),
        out_shape=jax.ShapeDtypeStruct((blocks, CH, CH * LAGS), BF16),
        in_specs=in_specs,
        out_specs=pl.BlockSpec(memory_space=pl.ANY),
        scratch_shapes=[
            pltpu.VMEM((count, CH, depth), BF16),
            pltpu.VMEM((count, 8, CH, 128), F32),
            pltpu.VMEM((count, coarse * CH, depth), BF16),
            pltpu.VMEM((js * fine, depth), BF16),
            pltpu.VMEM((js * fine, depth), BF16),
            pltpu.VMEM((coarse * CH, js * fine), F32),
            pltpu.VMEM((coarse * CH, js * fine), F32),
            pltpu.VMEM((count, CH, CH * LAGS), BF16),
            pltpu.SemaphoreType.DMA((count,)),
            pltpu.SemaphoreType.DMA((count, chunks)),
        ],
        input_output_aliases=aliases,
        compiler_params=pltpu.CompilerParams(vmem_limit_bytes=32 * 2**20),
        cost_estimate=pl.CostEstimate(
            flops=4 * count * CH * CH * LAGS * depth,
            bytes_accessed=2 * count * CH * CH * LAGS,
            transcendentals=0,
        ),
        name="lags_" + "_".join(str(s) for s in slots),
    )(*operands)


def body(strain, tile_pairs, tile_count):
    blocks = strain.shape[0] // CH
    wins = strain.shape[1]
    size = lax.axis_size("tile")
    depth = wins * 2 * BAND
    scale = 1.0 / math.sqrt(wins * BAND)
    table = jnp.asarray(dft_tables())
    ahead2 = [(i, i - 2) for i in range(2, size)]
    behind2 = [(i, i + 2) for i in range(size - 2)]
    across = [(i, i - 1) for i in range(2, size, 2)]
    swap = [(i, i ^ 1) for i in range(size)]

    view = strain.reshape(blocks * CH, wins, WIN // 128, 128).transpose(0, 2, 1, 3)
    view = view.reshape(blocks * CH, WIN // 128 * wins, 128)
    want = lax.ppermute(tile_pairs, "tile", behind2)[blocks - 1, 1]
    w0, w1, everything = spectra(view, table, blocks, wins)
    far0 = lax.ppermute(w0, "tile", ahead2)
    near1 = lax.ppermute(w1, "tile", across)
    other = lax.ppermute(everything, "tile", swap)
    far2 = lax.ppermute(chosen(want, everything, other), "tile", ahead2)
    shared = (scale, 4, tile_pairs, tile_count, everything, other)
    out = corr_tiles((0, 1), *shared, (far0, near1), None)
    return corr_tiles((2,), *shared, (far2,), out)


def solution(mesh):
    in_specs = (
        P(("groups", "tile"), None, None),
        P(("groups", "tile"), None),
        P(("groups", "tile")),
    )
    out_specs = P(("groups", "tile"), None, None)
    return jax.shard_map(body, mesh=mesh, in_specs=in_specs, out_specs=out_specs, check_vma=False)
```

```python
import functools
import math

import jax
import jax.numpy as jnp
import numpy as np
from jax import lax
from jax.experimental import pallas as pl
from jax.experimental.pallas import tpu as pltpu
from jax.sharding import PartitionSpec as P

CH = 128
WIN = 4096
BAND = 256
BIN0 = 60
SMOOTH = 64
LAGS = 64
ROWS = 16
PITCH = 72
BF16 = jnp.bfloat16
F32 = jnp.float32


def bin_order():
    return np.concatenate([np.arange(0, BAND, 2), np.arange(1, BAND, 2)])


def dft_tables():
    times = np.arange(WIN // 2, dtype=np.int64)[:, None]
    tables = []
    for parity in range(2):
        freqs = BIN0 + np.arange(parity, BAND, 2, dtype=np.int64)[None, :]
        angle = (times * freqs % WIN) * (2.0 * math.pi / WIN)
        tables.append(np.concatenate([np.cos(angle), -np.sin(angle)], 1))
    group = bin_order() // SMOOTH
    tables.append((group[:, None] == group[None, :]) / SMOOTH)
    return np.concatenate(tables, 0).astype(BF16)


def phase_tables(coarse, scale):
    fine = LAGS // coarse
    freqs = (BIN0 + bin_order())[None, :]
    lags_a = fine * np.arange(1, coarse // 2 + 1)[:, None]
    lags_b = np.arange(fine)[:, None]
    step = 2.0 * math.pi / WIN
    a = np.concatenate([np.cos(lags_a * freqs * step), np.sin(lags_a * freqs * step)], 1) * scale
    b = np.concatenate([np.cos(lags_b * freqs * step), np.sin(lags_b * freqs * step)], 1)
    return a.astype(np.float32), b.astype(np.float32)


def spectra_kernel(blocks, wins, x_hbm, tab_hbm, w0_ref, w1_ref, all_ref, x, tab, rows, left, x_sem, t_sem):
    part = CH // 2
    half = WIN // 2
    per = WIN // 128 * wins

    def x_copy(n):
        channels = pl.ds(n * part, part)
        return pltpu.make_async_copy(x_hbm.at[channels], x.at[channels], x_sem.at[n])

    t_copy = pltpu.make_async_copy(tab_hbm, tab, t_sem)
    x_copy(0).start()
    x_copy(1).start()
    t_copy.start()
    for n in range(2, 2 * blocks):
        x_copy(n).start()

    def fold(b, side):
        first = side * part
        for c in range(first, first + part):
            rows[c * PITCH : c * PITCH + per, :] = x[b * CH + c].astype(F32)
        for t in range(half // 128):
            for w in range(wins):
                row = first * PITCH + t * wins + w
                head = rows[pl.ds(row, part, stride=PITCH), :]
                tail = rows[pl.ds(row + per // 2, part, stride=PITCH), :]
                place = (slice(w * CH + first, w * CH + first + part), slice(t * 128, (t + 1) * 128))
                left[2 * b, place[0], place[1]] = (head + tail).astype(BF16)
                left[2 * b + 1, place[0], place[1]] = (head - tail).astype(BF16)

    def product(b, sign):
        table = tab[sign * half : (sign + 1) * half, :]
        return jnp.dot(left[2 * b + sign], table, preferred_element_type=F32)

    def finish(b, spec):
        mean = tab[2 * half :, :]
        energy = [s[:, :128] * s[:, :128] + s[:, 128:] * s[:, 128:] for s in spec]
        energy = jnp.concatenate(energy, 1)
        high = energy.astype(BF16)
        low = (energy - high.astype(F32)).astype(BF16)
        power = jnp.dot(high, mean, preferred_element_type=F32)
        power += jnp.dot(low, mean, preferred_element_type=F32)
        factor = lax.rsqrt(power + 1e-06)
        for w in range(wins):
            r = slice(w * CH, (w + 1) * CH)
            for q in range(4):
                sign, side = q % 2, q // 2
                value = spec[sign][r, side * 128 : (side + 1) * 128]
                value = (value * factor[r, sign * 128 : (sign + 1) * 128]).astype(BF16)
                column = (w * 4 + q) * 128
                all_ref[b, :, column : column + 128] = value
                if b < 2:
                    (w0_ref, w1_ref)[b][:, column : column + 128] = value

    x_copy(0).wait()
    fold(0, 0)
    x_copy(1).wait()
    fold(0, 1)
    t_copy.wait()
    for b in range(1, blocks):
        x_copy(2 * b).wait()
        x_copy(2 * b + 1).wait()
        even = product(b - 1, 0)
        fold(b, 0)
        odd = product(b - 1, 1)
        fold(b, 1)
        finish(b - 1, [even, odd])
    finish(blocks - 1, [product(blocks - 1, sign) for sign in range(2)])


def spectra(view, table, blocks, wins):
    depth = wins * 2 * BAND
    shapes = [(CH, depth), (CH, depth), (blocks, CH, depth)]
    return pl.pallas_call(
        functools.partial(spectra_kernel, blocks, wins),
        out_shape=[jax.ShapeDtypeStruct(shape, BF16) for shape in shapes],
        in_specs=[pl.BlockSpec(memory_space=pl.ANY)] * 2,
        out_specs=[pl.BlockSpec(memory_space=pltpu.VMEM)] * len(shapes),
        scratch_shapes=[
            pltpu.VMEM(view.shape, BF16),
            pltpu.VMEM(table.shape, BF16),
            pltpu.VMEM((CH * PITCH, 128), F32),
            pltpu.VMEM((2 * blocks, CH * wins, WIN // 2), BF16),
            pltpu.SemaphoreType.DMA((2 * blocks,)),
            pltpu.SemaphoreType.DMA,
        ],
        compiler_params=pltpu.CompilerParams(vmem_limit_bytes=52 * 2**20),
        cost_estimate=pl.CostEstimate(
            flops=2 * blocks * CH * wins * WIN * BAND,
            bytes_accessed=2 * blocks * CH * wins * WIN + 2 * WIN * BAND,
            transcendentals=0,
        ),
        name="spectra",
    )(view, table)


def chosen(want, everything, other):
    blocks = everything.shape[0]
    me = lax.axis_index("tile")
    index = want - me * blocks
    own = lax.dynamic_index_in_dim(everything, jnp.clip(index, 0, blocks - 1), 0, keepdims=False)
    beside = lax.dynamic_index_in_dim(
        other, jnp.clip(index + blocks, 0, blocks - 1), 0, keepdims=False
    )
    return jnp.where(jnp.logical_or(index >= 0, me % 2 == 0), own, beside)


def corr_kernel(slots, blocks, scale, coarse, *refs):
    fine = LAGS // coarse
    js = 256 // fine
    chunks = CH // js
    count = len(slots)
    pairs_ref, count_ref, atab_ref, btab_ref, all_ref, other_ref = refs[:6]
    fars = refs[6 : 6 + count]
    row_refs = refs[6 + count : 6 + 2 * count]
    out_hbm, raw, col, acoef, b0, b1, p0, p1, obuf, in_sem, out_sem = refs[-11:]
    me = lax.axis_index("tile")
    even = me % 2 == 0

    def out_copy(n, c):
        columns = pl.ds(c * js * LAGS, js * LAGS)
        return pltpu.make_async_copy(
            obuf.at[n, :, columns], out_hbm.at[slots[n], :, columns], out_sem.at[n, c]
        )

    def fetch(n):
        index = pairs_ref[slots[n], 1] - me * blocks
        own = index < blocks
        beside = jnp.logical_and(index >= blocks, jnp.logical_and(even, index < 2 * blocks))
        remote = jnp.logical_not(jnp.logical_or(own, beside))

        @pl.when(own)
        def _():
            source = all_ref.at[jnp.clip(index, 0, blocks - 1)]
            pltpu.make_async_copy(source, raw.at[n], in_sem.at[n]).start()

        @pl.when(beside)
        def _():
            source = other_ref.at[jnp.clip(index - blocks, 0, blocks - 1)]
            pltpu.make_async_copy(source, raw.at[n], in_sem.at[n]).start()

        @pl.when(remote)
        def _():
            pltpu.make_async_copy(fars[n], raw.at[n], in_sem.at[n]).start()

    def prepare(n):
        live = jnp.where(count_ref[0] > slots[n], 1.0, 0.0).astype(F32)
        for w in range(2):
            for p in range(2):
                re_cols = slice((w * 4 + p) * 128, (w * 4 + p + 1) * 128)
                im_cols = slice((w * 4 + 2 + p) * 128, (w * 4 + 3 + p) * 128)
                re = row_refs[n][0, :, re_cols].astype(F32)
                im = row_refs[n][0, :, im_cols].astype(F32)

                def put(a, re_value, im_value):
                    rows = slice(a * CH, (a + 1) * CH)
                    acoef[n, rows, re_cols] = re_value.astype(BF16)
                    acoef[n, rows, im_cols] = im_value.astype(BF16)

                middle = coarse // 2
                put(middle, re * (scale * live), im * (scale * live))
                for k in range(1, middle + 1):
                    cos = atab_ref[k - 1 : k, p * 128 : (p + 1) * 128] * live
                    sin = atab_ref[k - 1 : k, (2 + p) * 128 : (3 + p) * 128] * live
                    rc, ic, rs, ims = re * cos, im * cos, re * sin, im * sin
                    put(middle - k, rc + ims, ic - rs)
                    if k < middle:
                        put(middle + k, rc - ims, ic + rs)

    def build(n, c, b):
        for w in range(2):
            for p in range(2):
                re_q, im_q = w * 4 + p, w * 4 + 2 + p
                cos = btab_ref[:, p * 128 : (p + 1) * 128]
                sin = btab_ref[:, (2 + p) * 128 : (3 + p) * 128]
                step = max(ROWS // fine, 1)
                for place in range(0, js, step):
                    res, ims = [], []
                    for pos in range(place, place + step):
                        v, inner = divmod(pos, 2 * coarse)
                        jj, q = divmod(inner, coarse)
                        j = c * js + v * 2 * coarse + 2 * q + jj
                        re = col[n, re_q, pl.ds(j, 8, stride=0), :]
                        im = col[n, im_q, pl.ds(j, 8, stride=0), :]
                        re = jnp.concatenate([re] * (fine // 8), 0)
                        im = jnp.concatenate([im] * (fine // 8), 0)
                        res.append(re * cos + im * sin)
                        ims.append(im * cos - re * sin)
                    rows = slice(place * fine, (place + step) * fine)
                    b[rows, re_q * 128 : (re_q + 1) * 128] = jnp.concatenate(res, 0).astype(BF16)
                    b[rows, im_q * 128 : (im_q + 1) * 128] = jnp.concatenate(ims, 0).astype(BF16)

    def multiply(n, b, p):
        p[...] = lax.dot_general(
            acoef[n], b[...], (((1,), (1,)), ((), ())), preferred_element_type=F32
        )

    lane = lax.broadcasted_iota(jnp.int32, (CH, 128), 1)

    def arrange(n, c, prod):
        for v in range(2):
            x = [prod[a * CH : (a + 1) * CH, v * 128 : (v + 1) * 128] for a in range(coarse)]
            bit = 1
            while bit < coarse:
                upper = (lane // fine) & bit != 0
                for a in range(coarse):
                    if a & bit == 0:
                        lo, hi = x[a], x[a | bit]
                        x[a] = jnp.where(upper, pltpu.roll(hi, fine * bit, 1), lo)
                        x[a | bit] = jnp.where(upper, hi, pltpu.roll(lo, 128 - fine * bit, 1))
                bit *= 2
            for q in range(coarse):
                column = c * js * LAGS + (v * coarse + q) * 128
                obuf[n, :, column : column + 128] = x[q].astype(BF16)
        out_copy(n, c).start()

    def run():
        for n in range(count):
            fetch(n)
        prepare(0)
        for n in range(count):
            pltpu.make_async_copy(fars[n], raw.at[n], in_sem.at[n]).wait()
        bs, ps = (b0, b1), (p0, p1)
        steps = [(n, c) for n in range(count) for c in range(chunks)]

        def ready(k):
            n, c = steps[k]
            if c == 0:
                if n > 0:
                    prepare(n)
                for q in range(8):
                    col[n, q] = raw[n, :, q * 128 : (q + 1) * 128].astype(F32)
            build(n, c, bs[k % 2])

        ready(0)
        for k, (n, c) in enumerate(steps):
            multiply(n, bs[k % 2], ps[k % 2])
            if k > 0:
                arrange(*steps[k - 1], ps[(k - 1) % 2])
            if k + 1 < len(steps):
                ready(k + 1)
        arrange(*steps[-1], ps[(len(steps) - 1) % 2])

    if count == 1:
        live = count_ref[0] > slots[0]
        pl.when(live)(run)

        @pl.when(jnp.logical_not(live))
        def _():
            obuf[...] = jnp.zeros_like(obuf)
            for c in range(chunks):
                out_copy(0, c).start()
    else:
        run()
    for n in range(count):
        for c in range(chunks):
            out_copy(n, c).wait()


def corr_tiles(slots, scale, coarse, pairs, tile_count, everything, other, fars, buffer):
    fine = LAGS // coarse
    tables = [jnp.asarray(t) for t in phase_tables(coarse, scale)]
    js = 256 // fine
    chunks = CH // js
    count = len(slots)
    blocks, _, depth = everything.shape
    in_specs = [
        pl.BlockSpec(memory_space=pltpu.SMEM),
        pl.BlockSpec(memory_space=pltpu.SMEM),
        pl.BlockSpec(memory_space=pltpu.VMEM),
        pl.BlockSpec(memory_space=pltpu.VMEM),
    ] + [pl.BlockSpec(memory_space=pl.ANY)] * (2 + count)
    in_specs += [pl.BlockSpec((1, CH, depth), lambda i, s=s: (s, 0, 0)) for s in slots]
    operands = [pairs, tile_count, *tables, everything, other, *fars] + [everything] * count
    aliases = {}
    if buffer is not None:
        aliases = {len(operands): 0}
        operands.append(buffer)
        in_specs.append(pl.BlockSpec(memory_space=pl.ANY))
    return pl.pallas_call(
        functools.partial(corr_kernel, slots, blocks, scale, coarse),
        grid=(1,),
        out_shape=jax.ShapeDtypeStruct((blocks, CH, CH * LAGS), BF16),
        in_specs=in_specs,
        out_specs=pl.BlockSpec(memory_space=pl.ANY),
        scratch_shapes=[
            pltpu.VMEM((count, CH, depth), BF16),
            pltpu.VMEM((count, 8, CH, 128), F32),
            pltpu.VMEM((count, coarse * CH, depth), BF16),
            pltpu.VMEM((js * fine, depth), BF16),
            pltpu.VMEM((js * fine, depth), BF16),
            pltpu.VMEM((coarse * CH, js * fine), F32),
            pltpu.VMEM((coarse * CH, js * fine), F32),
            pltpu.VMEM((count, CH, CH * LAGS), BF16),
            pltpu.SemaphoreType.DMA((count,)),
            pltpu.SemaphoreType.DMA((count, chunks)),
        ],
        input_output_aliases=aliases,
        compiler_params=pltpu.CompilerParams(vmem_limit_bytes=32 * 2**20),
        cost_estimate=pl.CostEstimate(
            flops=4 * count * CH * CH * LAGS * depth,
            bytes_accessed=2 * count * CH * CH * LAGS,
            transcendentals=0,
        ),
        name="lags_" + "_".join(str(s) for s in slots),
    )(*operands)


def body(strain, tile_pairs, tile_count):
    blocks = strain.shape[0] // CH
    wins = strain.shape[1]
    size = lax.axis_size("tile")
    depth = wins * 2 * BAND
    scale = 1.0 / math.sqrt(wins * BAND)
    table = jnp.asarray(dft_tables())
    ahead2 = [(i, i - 2) for i in range(2, size)]
    behind2 = [(i, i + 2) for i in range(size - 2)]
    across = [(i, i - 1) for i in range(2, size, 2)]
    swap = [(i, i ^ 1) for i in range(size)]

    view = strain.reshape(blocks * CH, wins, WIN // 128, 128).transpose(0, 2, 1, 3)
    view = view.reshape(blocks * CH, WIN // 128 * wins, 128)
    want = lax.ppermute(tile_pairs, "tile", behind2)[blocks - 1, 1]
    w0, w1, everything = spectra(view, table, blocks, wins)
    far0 = lax.ppermute(w0, "tile", ahead2)
    near1 = lax.ppermute(w1, "tile", across)
    other = lax.ppermute(everything, "tile", swap)
    far2 = lax.ppermute(chosen(want, everything, other), "tile", ahead2)
    shared = (scale, 4, tile_pairs, tile_count, everything, other)
    out = corr_tiles((0, 1), *shared, (far0, near1), None)
    return corr_tiles((2,), *shared, (far2,), out)


def solution(mesh):
    in_specs = (
        P(("groups", "tile"), None, None),
        P(("groups", "tile"), None),
        P(("groups", "tile")),
    )
    out_specs = P(("groups", "tile"), None, None)
    return jax.shard_map(body, mesh=mesh, in_specs=in_specs, out_specs=out_specs, check_vma=False)
```

```python
import functools
import math

import jax
import jax.numpy as jnp
import numpy as np
from jax import lax
from jax.experimental import pallas as pl
from jax.experimental.pallas import tpu as pltpu
from jax.sharding import PartitionSpec as P

CH = 128
WIN = 4096
BAND = 256
BIN0 = 60
SMOOTH = 64
LAGS = 64
ROWS = 16
PITCH = 72
BF16 = jnp.bfloat16
F32 = jnp.float32


def bin_order():
    return np.concatenate([np.arange(0, BAND, 2), np.arange(1, BAND, 2)])


def dft_tables():
    times = np.arange(WIN // 2, dtype=np.int64)[:, None]
    tables = []
    for parity in range(2):
        freqs = BIN0 + np.arange(parity, BAND, 2, dtype=np.int64)[None, :]
        angle = (times * freqs % WIN) * (2.0 * math.pi / WIN)
        tables.append(np.concatenate([np.cos(angle), -np.sin(angle)], 1))
    group = bin_order() // SMOOTH
    tables.append((group[:, None] == group[None, :]) / SMOOTH)
    return np.concatenate(tables, 0).astype(BF16)


def phase_tables(coarse, scale):
    fine = LAGS // coarse
    freqs = (BIN0 + bin_order())[None, :]
    lags_a = fine * np.arange(1, coarse // 2 + 1)[:, None]
    lags_b = np.arange(fine)[:, None]
    step = 2.0 * math.pi / WIN
    a = np.concatenate([np.cos(lags_a * freqs * step), np.sin(lags_a * freqs * step)], 1) * scale
    b = np.concatenate([np.cos(lags_b * freqs * step), np.sin(lags_b * freqs * step)], 1)
    return a.astype(np.float32), b.astype(np.float32)


def spectra_kernel(blocks, wins, x_hbm, tab_hbm, w0_ref, w1_ref, all_ref, x, tab, rows, left, x_sem, t_sem):
    part = CH // 2
    half = WIN // 2
    per = WIN // 128 * wins

    def x_copy(n):
        channels = pl.ds(n * part, part)
        return pltpu.make_async_copy(x_hbm.at[channels], x.at[channels], x_sem.at[n])

    t_copy = pltpu.make_async_copy(tab_hbm, tab, t_sem)
    x_copy(0).start()
    x_copy(1).start()
    t_copy.start()
    for n in range(2, 2 * blocks):
        x_copy(n).start()

    def fold(b, side):
        first = side * part
        for c in range(first, first + part):
            rows[c * PITCH : c * PITCH + per, :] = x[b * CH + c].astype(F32)
        for t in range(half // 128):
            for w in range(wins):
                row = first * PITCH + t * wins + w
                head = rows[pl.ds(row, part, stride=PITCH), :]
                tail = rows[pl.ds(row + per // 2, part, stride=PITCH), :]
                place = (slice(w * CH + first, w * CH + first + part), slice(t * 128, (t + 1) * 128))
                left[2 * b, place[0], place[1]] = (head + tail).astype(BF16)
                left[2 * b + 1, place[0], place[1]] = (head - tail).astype(BF16)

    def product(b, sign):
        table = tab[sign * half : (sign + 1) * half, :]
        return jnp.dot(left[2 * b + sign], table, preferred_element_type=F32)

    def finish(b, spec):
        mean = tab[2 * half :, :]
        energy = [s[:, :128] * s[:, :128] + s[:, 128:] * s[:, 128:] for s in spec]
        energy = jnp.concatenate(energy, 1)
        high = energy.astype(BF16)
        low = (energy - high.astype(F32)).astype(BF16)
        power = jnp.dot(high, mean, preferred_element_type=F32)
        power += jnp.dot(low, mean, preferred_element_type=F32)
        factor = lax.rsqrt(power + 1e-06)
        for w in range(wins):
            r = slice(w * CH, (w + 1) * CH)
            for q in range(4):
                sign, side = q % 2, q // 2
                value = spec[sign][r, side * 128 : (side + 1) * 128]
                value = (value * factor[r, sign * 128 : (sign + 1) * 128]).astype(BF16)
                column = (w * 4 + q) * 128
                all_ref[b, :, column : column + 128] = value
                if b < 2:
                    (w0_ref, w1_ref)[b][:, column : column + 128] = value

    x_copy(0).wait()
    fold(0, 0)
    x_copy(1).wait()
    fold(0, 1)
    t_copy.wait()
    for b in range(1, blocks):
        x_copy(2 * b).wait()
        x_copy(2 * b + 1).wait()
        even = product(b - 1, 0)
        fold(b, 0)
        odd = product(b - 1, 1)
        fold(b, 1)
        finish(b - 1, [even, odd])
    finish(blocks - 1, [product(blocks - 1, sign) for sign in range(2)])


def spectra(view, table, blocks, wins):
    depth = wins * 2 * BAND
    shapes = [(CH, depth), (CH, depth), (blocks, CH, depth)]
    return pl.pallas_call(
        functools.partial(spectra_kernel, blocks, wins),
        out_shape=[jax.ShapeDtypeStruct(shape, BF16) for shape in shapes],
        in_specs=[pl.BlockSpec(memory_space=pl.ANY)] * 2,
        out_specs=[pl.BlockSpec(memory_space=pltpu.VMEM)] * len(shapes),
        scratch_shapes=[
            pltpu.VMEM(view.shape, BF16),
            pltpu.VMEM(table.shape, BF16),
            pltpu.VMEM((CH * PITCH, 128), F32),
            pltpu.VMEM((2 * blocks, CH * wins, WIN // 2), BF16),
            pltpu.SemaphoreType.DMA((2 * blocks,)),
            pltpu.SemaphoreType.DMA,
        ],
        compiler_params=pltpu.CompilerParams(vmem_limit_bytes=52 * 2**20),
        cost_estimate=pl.CostEstimate(
            flops=2 * blocks * CH * wins * WIN * BAND,
            bytes_accessed=2 * blocks * CH * wins * WIN + 2 * WIN * BAND,
            transcendentals=0,
        ),
        name="spectra",
    )(view, table)


def chosen(want, everything, other):
    blocks = everything.shape[0]
    me = lax.axis_index("tile")
    index = want - me * blocks
    own = lax.dynamic_index_in_dim(everything, jnp.clip(index, 0, blocks - 1), 0, keepdims=False)
    beside = lax.dynamic_index_in_dim(
        other, jnp.clip(index + blocks, 0, blocks - 1), 0, keepdims=False
    )
    return jnp.where(jnp.logical_or(index >= 0, me % 2 == 0), own, beside)


def corr_kernel(slots, blocks, scale, coarse, width, *refs):
    fine = LAGS // coarse
    js = width // fine
    chunks = CH // js
    count = len(slots)
    pairs_ref, count_ref, atab_ref, btab_ref, all_ref, other_ref = refs[:6]
    fars = refs[6 : 6 + count]
    row_refs = refs[6 + count : 6 + 2 * count]
    out_hbm, raw, col, acoef, b0, b1, p0, p1, obuf, in_sem, out_sem = refs[-11:]
    me = lax.axis_index("tile")
    even = me % 2 == 0

    def out_copy(n, c):
        columns = pl.ds(c * js * LAGS, js * LAGS)
        return pltpu.make_async_copy(
            obuf.at[n, :, columns], out_hbm.at[slots[n], :, columns], out_sem.at[n, c]
        )

    def fetch(n):
        index = pairs_ref[slots[n], 1] - me * blocks
        own = index < blocks
        beside = jnp.logical_and(index >= blocks, jnp.logical_and(even, index < 2 * blocks))
        remote = jnp.logical_not(jnp.logical_or(own, beside))

        @pl.when(own)
        def _():
            source = all_ref.at[jnp.clip(index, 0, blocks - 1)]
            pltpu.make_async_copy(source, raw.at[n], in_sem.at[n]).start()

        @pl.when(beside)
        def _():
            source = other_ref.at[jnp.clip(index - blocks, 0, blocks - 1)]
            pltpu.make_async_copy(source, raw.at[n], in_sem.at[n]).start()

        @pl.when(remote)
        def _():
            pltpu.make_async_copy(fars[n], raw.at[n], in_sem.at[n]).start()

    def prepare(n):
        live = jnp.where(count_ref[0] > slots[n], 1.0, 0.0).astype(F32)
        for w in range(2):
            for p in range(2):
                re_cols = slice((w * 4 + p) * 128, (w * 4 + p + 1) * 128)
                im_cols = slice((w * 4 + 2 + p) * 128, (w * 4 + 3 + p) * 128)
                re = row_refs[n][0, :, re_cols].astype(F32)
                im = row_refs[n][0, :, im_cols].astype(F32)

                def put(a, re_value, im_value):
                    rows = slice(a * CH, (a + 1) * CH)
                    acoef[n, rows, re_cols] = re_value.astype(BF16)
                    acoef[n, rows, im_cols] = im_value.astype(BF16)

                middle = coarse // 2
                put(middle, re * (scale * live), im * (scale * live))
                for k in range(1, middle + 1):
                    cos = atab_ref[k - 1 : k, p * 128 : (p + 1) * 128] * live
                    sin = atab_ref[k - 1 : k, (2 + p) * 128 : (3 + p) * 128] * live
                    rc, ic, rs, ims = re * cos, im * cos, re * sin, im * sin
                    put(middle - k, rc + ims, ic - rs)
                    if k < middle:
                        put(middle + k, rc - ims, ic + rs)

    def build(n, c, b):
        for w in range(2):
            for p in range(2):
                re_q, im_q = w * 4 + p, w * 4 + 2 + p
                cos = btab_ref[:, p * 128 : (p + 1) * 128]
                sin = btab_ref[:, (2 + p) * 128 : (3 + p) * 128]
                step = max(ROWS // fine, 1)
                for place in range(0, js, step):
                    res, ims = [], []
                    for pos in range(place, place + step):
                        v, inner = divmod(pos, 2 * coarse)
                        jj, q = divmod(inner, coarse)
                        j = c * js + v * 2 * coarse + 2 * q + jj
                        re = col[n, re_q, pl.ds(j, 8, stride=0), :]
                        im = col[n, im_q, pl.ds(j, 8, stride=0), :]
                        re = jnp.concatenate([re] * (fine // 8), 0)
                        im = jnp.concatenate([im] * (fine // 8), 0)
                        res.append(re * cos + im * sin)
                        ims.append(im * cos - re * sin)
                    rows = slice(place * fine, (place + step) * fine)
                    b[rows, re_q * 128 : (re_q + 1) * 128] = jnp.concatenate(res, 0).astype(BF16)
                    b[rows, im_q * 128 : (im_q + 1) * 128] = jnp.concatenate(ims, 0).astype(BF16)

    def multiply(n, b, p):
        p[...] = lax.dot_general(
            acoef[n], b[...], (((1,), (1,)), ((), ())), preferred_element_type=F32
        )

    lane = lax.broadcasted_iota(jnp.int32, (CH, 128), 1)

    def arrange(n, c, prod):
        for v in range(width // 128):
            x = [prod[a * CH : (a + 1) * CH, v * 128 : (v + 1) * 128] for a in range(coarse)]
            bit = 1
            while bit < coarse:
                upper = (lane // fine) & bit != 0
                for a in range(coarse):
                    if a & bit == 0:
                        lo, hi = x[a], x[a | bit]
                        x[a] = jnp.where(upper, pltpu.roll(hi, fine * bit, 1), lo)
                        x[a | bit] = jnp.where(upper, hi, pltpu.roll(lo, 128 - fine * bit, 1))
                bit *= 2
            for q in range(coarse):
                column = c * js * LAGS + (v * coarse + q) * 128
                obuf[n, :, column : column + 128] = x[q].astype(BF16)
        out_copy(n, c).start()

    def run():
        for n in range(count):
            fetch(n)
        prepare(0)
        for n in range(count):
            pltpu.make_async_copy(fars[n], raw.at[n], in_sem.at[n]).wait()
        bs, ps = (b0, b1), (p0, p1)
        steps = [(n, c) for n in range(count) for c in range(chunks)]

        def ready(k):
            n, c = steps[k]
            if c == 0:
                if n > 0:
                    prepare(n)
                for q in range(8):
                    col[n, q] = raw[n, :, q * 128 : (q + 1) * 128].astype(F32)
            build(n, c, bs[k % 2])

        ready(0)
        for k, (n, c) in enumerate(steps):
            multiply(n, bs[k % 2], ps[k % 2])
            if k > 0:
                arrange(*steps[k - 1], ps[(k - 1) % 2])
            if k + 1 < len(steps):
                ready(k + 1)
        arrange(*steps[-1], ps[(len(steps) - 1) % 2])

    if count == 1:
        live = count_ref[0] > slots[0]
        pl.when(live)(run)

        @pl.when(jnp.logical_not(live))
        def _():
            obuf[...] = jnp.zeros_like(obuf)
            for c in range(chunks):
                out_copy(0, c).start()
    else:
        run()
    for n in range(count):
        for c in range(chunks):
            out_copy(n, c).wait()


def corr_tiles(slots, width, scale, coarse, pairs, tile_count, everything, other, fars, buffer):
    fine = LAGS // coarse
    tables = [jnp.asarray(t) for t in phase_tables(coarse, scale)]
    js = width // fine
    chunks = CH // js
    count = len(slots)
    blocks, _, depth = everything.shape
    in_specs = [
        pl.BlockSpec(memory_space=pltpu.SMEM),
        pl.BlockSpec(memory_space=pltpu.SMEM),
        pl.BlockSpec(memory_space=pltpu.VMEM),
        pl.BlockSpec(memory_space=pltpu.VMEM),
    ] + [pl.BlockSpec(memory_space=pl.ANY)] * (2 + count)
    in_specs += [pl.BlockSpec((1, CH, depth), lambda i, s=s: (s, 0, 0)) for s in slots]
    operands = [pairs, tile_count, *tables, everything, other, *fars] + [everything] * count
    aliases = {}
    if buffer is not None:
        aliases = {len(operands): 0}
        operands.append(buffer)
        in_specs.append(pl.BlockSpec(memory_space=pl.ANY))
    return pl.pallas_call(
        functools.partial(corr_kernel, slots, blocks, scale, coarse, width),
        grid=(1,),
        out_shape=jax.ShapeDtypeStruct((blocks, CH, CH * LAGS), BF16),
        in_specs=in_specs,
        out_specs=pl.BlockSpec(memory_space=pl.ANY),
        scratch_shapes=[
            pltpu.VMEM((count, CH, depth), BF16),
            pltpu.VMEM((count, 8, CH, 128), F32),
            pltpu.VMEM((count, coarse * CH, depth), BF16),
            pltpu.VMEM((js * fine, depth), BF16),
            pltpu.VMEM((js * fine, depth), BF16),
            pltpu.VMEM((coarse * CH, js * fine), F32),
            pltpu.VMEM((coarse * CH, js * fine), F32),
            pltpu.VMEM((count, CH, CH * LAGS), BF16),
            pltpu.SemaphoreType.DMA((count,)),
            pltpu.SemaphoreType.DMA((count, chunks)),
        ],
        input_output_aliases=aliases,
        compiler_params=pltpu.CompilerParams(vmem_limit_bytes=32 * 2**20),
        cost_estimate=pl.CostEstimate(
            flops=4 * count * CH * CH * LAGS * depth,
            bytes_accessed=2 * count * CH * CH * LAGS,
            transcendentals=0,
        ),
        name="lags_" + "_".join(str(s) for s in slots),
    )(*operands)


def body(strain, tile_pairs, tile_count):
    blocks = strain.shape[0] // CH
    wins = strain.shape[1]
    size = lax.axis_size("tile")
    depth = wins * 2 * BAND
    scale = 1.0 / math.sqrt(wins * BAND)
    table = jnp.asarray(dft_tables())
    ahead2 = [(i, i - 2) for i in range(2, size)]
    behind2 = [(i, i + 2) for i in range(size - 2)]
    across = [(i, i - 1) for i in range(2, size, 2)]
    swap = [(i, i ^ 1) for i in range(size)]

    view = strain.reshape(blocks * CH, wins, WIN // 128, 128).transpose(0, 2, 1, 3)
    view = view.reshape(blocks * CH, WIN // 128 * wins, 128)
    want = lax.ppermute(tile_pairs, "tile", behind2)[blocks - 1, 1]
    w0, w1, everything = spectra(view, table, blocks, wins)
    far0 = lax.ppermute(w0, "tile", ahead2)
    near1 = lax.ppermute(w1, "tile", across)
    other = lax.ppermute(everything, "tile", swap)
    far2 = lax.ppermute(chosen(want, everything, other), "tile", ahead2)
    shared = (scale, 4, tile_pairs, tile_count, everything, other)
    out = corr_tiles((0, 1), 512, *shared, (far0, near1), None)
    return corr_tiles((2,), 256, *shared, (far2,), out)


def solution(mesh):
    in_specs = (
        P(("groups", "tile"), None, None),
        P(("groups", "tile"), None),
        P(("groups", "tile")),
    )
    out_specs = P(("groups", "tile"), None, None)
    return jax.shard_map(body, mesh=mesh, in_specs=in_specs, out_specs=out_specs, check_vma=False)
```

```python
import functools
import math

import jax
import jax.numpy as jnp
import numpy as np
from jax import lax
from jax.experimental import pallas as pl
from jax.experimental.pallas import tpu as pltpu
from jax.sharding import PartitionSpec as P

CH = 128
WIN = 4096
BAND = 256
BIN0 = 60
SMOOTH = 64
LAGS = 64
ROWS = 16
PITCH = 72
BF16 = jnp.bfloat16
F32 = jnp.float32


def bin_order():
    return np.concatenate([np.arange(0, BAND, 2), np.arange(1, BAND, 2)])


def dft_tables():
    times = np.arange(WIN // 2, dtype=np.int64)[:, None]
    tables = []
    for parity in range(2):
        freqs = BIN0 + np.arange(parity, BAND, 2, dtype=np.int64)[None, :]
        angle = (times * freqs % WIN) * (2.0 * math.pi / WIN)
        tables.append(np.concatenate([np.cos(angle), -np.sin(angle)], 1))
    group = bin_order() // SMOOTH
    tables.append((group[:, None] == group[None, :]) / SMOOTH)
    return np.concatenate(tables, 0).astype(BF16)


def phase_tables(coarse, scale):
    fine = LAGS // coarse
    freqs = (BIN0 + bin_order())[None, :]
    lags_a = fine * np.arange(1, coarse // 2 + 1)[:, None]
    lags_b = np.arange(fine)[:, None]
    step = 2.0 * math.pi / WIN
    a = np.concatenate([np.cos(lags_a * freqs * step), np.sin(lags_a * freqs * step)], 1) * scale
    b = np.concatenate([np.cos(lags_b * freqs * step), np.sin(lags_b * freqs * step)], 1)
    return a.astype(np.float32), b.astype(np.float32)


def spectra_kernel(blocks, wins, x_hbm, tab_hbm, w0_ref, w1_ref, all_ref, x, tab, rows, left, x_sem, t_sem):
    part = CH // 2
    half = WIN // 2
    per = WIN // 128 * wins

    def x_copy(n):
        channels = pl.ds(n * part, part)
        return pltpu.make_async_copy(x_hbm.at[channels], x.at[channels], x_sem.at[n])

    t_copy = pltpu.make_async_copy(tab_hbm, tab, t_sem)
    x_copy(0).start()
    x_copy(1).start()
    t_copy.start()
    for n in range(2, 2 * blocks):
        x_copy(n).start()

    def fold(b, side):
        first = side * part
        for c in range(first, first + part):
            rows[c * PITCH : c * PITCH + per, :] = x[b * CH + c].astype(F32)
        for t in range(half // 128):
            for w in range(wins):
                row = first * PITCH + t * wins + w
                head = rows[pl.ds(row, part, stride=PITCH), :]
                tail = rows[pl.ds(row + per // 2, part, stride=PITCH), :]
                place = (slice(w * CH + first, w * CH + first + part), slice(t * 128, (t + 1) * 128))
                left[2 * b, place[0], place[1]] = (head + tail).astype(BF16)
                left[2 * b + 1, place[0], place[1]] = (head - tail).astype(BF16)

    def product(b, sign):
        table = tab[sign * half : (sign + 1) * half, :]
        return jnp.dot(left[2 * b + sign], table, preferred_element_type=F32)

    def finish(b, spec):
        mean = tab[2 * half :, :]
        energy = [s[:, :128] * s[:, :128] + s[:, 128:] * s[:, 128:] for s in spec]
        energy = jnp.concatenate(energy, 1)
        high = energy.astype(BF16)
        low = (energy - high.astype(F32)).astype(BF16)
        power = jnp.dot(high, mean, preferred_element_type=F32)
        power += jnp.dot(low, mean, preferred_element_type=F32)
        factor = lax.rsqrt(power + 1e-06)
        for w in range(wins):
            r = slice(w * CH, (w + 1) * CH)
            for q in range(4):
                sign, side = q % 2, q // 2
                value = spec[sign][r, side * 128 : (side + 1) * 128]
                value = (value * factor[r, sign * 128 : (sign + 1) * 128]).astype(BF16)
                column = (w * 4 + q) * 128
                all_ref[b, :, column : column + 128] = value
                if b < 2:
                    (w0_ref, w1_ref)[b][:, column : column + 128] = value

    x_copy(0).wait()
    fold(0, 0)
    x_copy(1).wait()
    fold(0, 1)
    t_copy.wait()
    for b in range(1, blocks):
        x_copy(2 * b).wait()
        x_copy(2 * b + 1).wait()
        even = product(b - 1, 0)
        fold(b, 0)
        odd = product(b - 1, 1)
        fold(b, 1)
        finish(b - 1, [even, odd])
    finish(blocks - 1, [product(blocks - 1, sign) for sign in range(2)])


def spectra(view, table, blocks, wins):
    depth = wins * 2 * BAND
    shapes = [(CH, depth), (CH, depth), (blocks, CH, depth)]
    return pl.pallas_call(
        functools.partial(spectra_kernel, blocks, wins),
        out_shape=[jax.ShapeDtypeStruct(shape, BF16) for shape in shapes],
        in_specs=[pl.BlockSpec(memory_space=pl.ANY)] * 2,
        out_specs=[pl.BlockSpec(memory_space=pltpu.VMEM)] * len(shapes),
        scratch_shapes=[
            pltpu.VMEM(view.shape, BF16),
            pltpu.VMEM(table.shape, BF16),
            pltpu.VMEM((CH * PITCH, 128), F32),
            pltpu.VMEM((2 * blocks, CH * wins, WIN // 2), BF16),
            pltpu.SemaphoreType.DMA((2 * blocks,)),
            pltpu.SemaphoreType.DMA,
        ],
        compiler_params=pltpu.CompilerParams(vmem_limit_bytes=52 * 2**20),
        cost_estimate=pl.CostEstimate(
            flops=2 * blocks * CH * wins * WIN * BAND,
            bytes_accessed=2 * blocks * CH * wins * WIN + 2 * WIN * BAND,
            transcendentals=0,
        ),
        name="spectra",
    )(view, table)


def chosen(want, everything, other):
    blocks = everything.shape[0]
    me = lax.axis_index("tile")
    index = want - me * blocks
    own = lax.dynamic_index_in_dim(everything, jnp.clip(index, 0, blocks - 1), 0, keepdims=False)
    beside = lax.dynamic_index_in_dim(
        other, jnp.clip(index + blocks, 0, blocks - 1), 0, keepdims=False
    )
    return jnp.where(jnp.logical_or(index >= 0, me % 2 == 0), own, beside)


def corr_kernel(slots, blocks, scale, coarse, width, *refs):
    fine = LAGS // coarse
    js = width // fine
    chunks = CH // js
    count = len(slots)
    pairs_ref, count_ref, atab_ref, btab_ref, all_ref, other_ref = refs[:6]
    fars = refs[6 : 6 + count]
    row_refs = refs[6 + count : 6 + 2 * count]
    out_hbm, raw, col, acoef, b0, b1, p0, p1, obuf, in_sem, out_sem = refs[-11:]
    me = lax.axis_index("tile")
    even = me % 2 == 0

    def out_copy(n, c):
        columns = pl.ds(c * js * LAGS, js * LAGS)
        return pltpu.make_async_copy(
            obuf.at[n, :, columns], out_hbm.at[slots[n], :, columns], out_sem.at[n, c]
        )

    def fetch(n):
        index = pairs_ref[slots[n], 1] - me * blocks
        own = index < blocks
        beside = jnp.logical_and(index >= blocks, jnp.logical_and(even, index < 2 * blocks))
        remote = jnp.logical_not(jnp.logical_or(own, beside))

        @pl.when(own)
        def _():
            source = all_ref.at[jnp.clip(index, 0, blocks - 1)]
            pltpu.make_async_copy(source, raw.at[n], in_sem.at[n]).start()

        @pl.when(beside)
        def _():
            source = other_ref.at[jnp.clip(index - blocks, 0, blocks - 1)]
            pltpu.make_async_copy(source, raw.at[n], in_sem.at[n]).start()

        @pl.when(remote)
        def _():
            pltpu.make_async_copy(fars[n], raw.at[n], in_sem.at[n]).start()

    def prepare(n):
        live = jnp.where(count_ref[0] > slots[n], 1.0, 0.0).astype(F32)
        for w in range(2):
            for p in range(2):
                re_cols = slice((w * 4 + p) * 128, (w * 4 + p + 1) * 128)
                im_cols = slice((w * 4 + 2 + p) * 128, (w * 4 + 3 + p) * 128)
                re = row_refs[n][0, :, re_cols].astype(F32)
                im = row_refs[n][0, :, im_cols].astype(F32)

                def put(a, re_value, im_value):
                    rows = slice(a * CH, (a + 1) * CH)
                    acoef[n, rows, re_cols] = re_value.astype(BF16)
                    acoef[n, rows, im_cols] = im_value.astype(BF16)

                middle = coarse // 2
                put(middle, re * (scale * live), im * (scale * live))
                for k in range(1, middle + 1):
                    cos = atab_ref[k - 1 : k, p * 128 : (p + 1) * 128] * live
                    sin = atab_ref[k - 1 : k, (2 + p) * 128 : (3 + p) * 128] * live
                    rc, ic, rs, ims = re * cos, im * cos, re * sin, im * sin
                    put(middle - k, rc + ims, ic - rs)
                    if k < middle:
                        put(middle + k, rc - ims, ic + rs)

    def build(n, c, b):
        for w in range(2):
            for p in range(2):
                re_q, im_q = w * 4 + p, w * 4 + 2 + p
                cos = btab_ref[:, p * 128 : (p + 1) * 128]
                sin = btab_ref[:, (2 + p) * 128 : (3 + p) * 128]
                step = max(ROWS // fine, 1)
                for place in range(0, js, step):
                    res, ims = [], []
                    for pos in range(place, place + step):
                        v, inner = divmod(pos, 2 * coarse)
                        jj, q = divmod(inner, coarse)
                        j = c * js + v * 2 * coarse + 2 * q + jj
                        re = col[n, re_q, pl.ds(j, 8, stride=0), :]
                        im = col[n, im_q, pl.ds(j, 8, stride=0), :]
                        re = jnp.concatenate([re] * (fine // 8), 0)
                        im = jnp.concatenate([im] * (fine // 8), 0)
                        res.append(re * cos + im * sin)
                        ims.append(im * cos - re * sin)
                    rows = slice(place * fine, (place + step) * fine)
                    b[rows, re_q * 128 : (re_q + 1) * 128] = jnp.concatenate(res, 0).astype(BF16)
                    b[rows, im_q * 128 : (im_q + 1) * 128] = jnp.concatenate(ims, 0).astype(BF16)

    def multiply(n, b, p):
        p[...] = lax.dot_general(
            acoef[n], b[...], (((1,), (1,)), ((), ())), preferred_element_type=F32
        )

    lane = lax.broadcasted_iota(jnp.int32, (CH, 128), 1)

    def arrange(n, c, prod):
        for v in range(width // 128):
            x = [prod[a * CH : (a + 1) * CH, v * 128 : (v + 1) * 128] for a in range(coarse)]
            bit = 1
            while bit < coarse:
                upper = (lane // fine) & bit != 0
                for a in range(coarse):
                    if a & bit == 0:
                        lo, hi = x[a], x[a | bit]
                        x[a] = jnp.where(upper, pltpu.roll(hi, fine * bit, 1), lo)
                        x[a | bit] = jnp.where(upper, hi, pltpu.roll(lo, 128 - fine * bit, 1))
                bit *= 2
            for q in range(coarse):
                column = c * js * LAGS + (v * coarse + q) * 128
                obuf[n, :, column : column + 128] = x[q].astype(BF16)
        out_copy(n, c).start()

    def run():
        for n in range(count):
            fetch(n)
        prepare(0)
        for n in range(count):
            pltpu.make_async_copy(fars[n], raw.at[n], in_sem.at[n]).wait()
        bs, ps = (b0, b1), (p0, p1)
        steps = [(n, c) for n in range(count) for c in range(chunks)]

        def ready(k):
            n, c = steps[k]
            if c == 0:
                if n > 0:
                    prepare(n)
                for q in range(8):
                    col[n, q] = raw[n, :, q * 128 : (q + 1) * 128].astype(F32)
            build(n, c, bs[k % 2])

        ready(0)
        for k, (n, c) in enumerate(steps):
            multiply(n, bs[k % 2], ps[k % 2])
            if k > 0:
                arrange(*steps[k - 1], ps[(k - 1) % 2])
            if k + 1 < len(steps):
                ready(k + 1)
        arrange(*steps[-1], ps[(len(steps) - 1) % 2])

    if count == 1:
        live = count_ref[0] > slots[0]
        pl.when(live)(run)

        @pl.when(jnp.logical_not(live))
        def _():
            obuf[...] = jnp.zeros_like(obuf)
            for c in range(chunks):
                out_copy(0, c).start()
    else:
        run()
    for n in range(count):
        for c in range(chunks):
            out_copy(n, c).wait()


def corr_tiles(slots, width, scale, coarse, pairs, tile_count, everything, other, fars, buffer):
    fine = LAGS // coarse
    tables = [jnp.asarray(t) for t in phase_tables(coarse, scale)]
    js = width // fine
    chunks = CH // js
    count = len(slots)
    blocks, _, depth = everything.shape
    in_specs = [
        pl.BlockSpec(memory_space=pltpu.SMEM),
        pl.BlockSpec(memory_space=pltpu.SMEM),
        pl.BlockSpec(memory_space=pltpu.VMEM),
        pl.BlockSpec(memory_space=pltpu.VMEM),
    ] + [pl.BlockSpec(memory_space=pl.ANY)] * (2 + count)
    in_specs += [pl.BlockSpec((1, CH, depth), lambda i, s=s: (s, 0, 0)) for s in slots]
    operands = [pairs, tile_count, *tables, everything, other, *fars] + [everything] * count
    aliases = {}
    if buffer is not None:
        aliases = {len(operands): 0}
        operands.append(buffer)
        in_specs.append(pl.BlockSpec(memory_space=pl.ANY))
    return pl.pallas_call(
        functools.partial(corr_kernel, slots, blocks, scale, coarse, width),
        grid=(1,),
        out_shape=jax.ShapeDtypeStruct((blocks, CH, CH * LAGS), BF16),
        in_specs=in_specs,
        out_specs=pl.BlockSpec(memory_space=pl.ANY),
        scratch_shapes=[
            pltpu.VMEM((count, CH, depth), BF16),
            pltpu.VMEM((count, 8, CH, 128), F32),
            pltpu.VMEM((count, coarse * CH, depth), BF16),
            pltpu.VMEM((js * fine, depth), BF16),
            pltpu.VMEM((js * fine, depth), BF16),
            pltpu.VMEM((coarse * CH, js * fine), F32),
            pltpu.VMEM((coarse * CH, js * fine), F32),
            pltpu.VMEM((count, CH, CH * LAGS), BF16),
            pltpu.SemaphoreType.DMA((count,)),
            pltpu.SemaphoreType.DMA((count, chunks)),
        ],
        input_output_aliases=aliases,
        compiler_params=pltpu.CompilerParams(vmem_limit_bytes=32 * 2**20),
        cost_estimate=pl.CostEstimate(
            flops=4 * count * CH * CH * LAGS * depth,
            bytes_accessed=2 * count * CH * CH * LAGS,
            transcendentals=0,
        ),
        name="lags_" + "_".join(str(s) for s in slots),
    )(*operands)


def body(strain, tile_pairs, tile_count):
    blocks = strain.shape[0] // CH
    wins = strain.shape[1]
    size = lax.axis_size("tile")
    depth = wins * 2 * BAND
    scale = 1.0 / math.sqrt(wins * BAND)
    table = jnp.asarray(dft_tables())
    ahead2 = [(i, i - 2) for i in range(2, size)]
    behind2 = [(i, i + 2) for i in range(size - 2)]
    across = [(i, i - 1) for i in range(2, size, 2)]
    swap = [(i, i ^ 1) for i in range(size)]

    view = strain.reshape(blocks * CH, wins, WIN // 128, 128).transpose(0, 2, 1, 3)
    view = view.reshape(blocks * CH, WIN // 128 * wins, 128)
    want = lax.ppermute(tile_pairs, "tile", behind2)[blocks - 1, 1]
    w0, w1, everything = spectra(view, table, blocks, wins)
    far0 = lax.ppermute(w0, "tile", ahead2)
    near1 = lax.ppermute(w1, "tile", across)
    other = lax.ppermute(everything, "tile", swap)
    far2 = lax.ppermute(chosen(want, everything, other), "tile", ahead2)
    shared = (scale, 4, tile_pairs, tile_count, everything, other)
    out = corr_tiles((0, 1), 512, *shared, (far0, near1), None)
    return corr_tiles((2,), 512, *shared, (far2,), out)


def solution(mesh):
    in_specs = (
        P(("groups", "tile"), None, None),
        P(("groups", "tile"), None),
        P(("groups", "tile")),
    )
    out_specs = P(("groups", "tile"), None, None)
    return jax.shard_map(body, mesh=mesh, in_specs=in_specs, out_specs=out_specs, check_vma=False)
```
